32 devices in a mesh: dp: 32 (over z, y, x, core).
Axes of the slice: x: 2, y: 2, z: 4, core: 2. Of those that a mesh axis runs over, the one named last changes fastest.
Arguments:
- tokens: bfloat16 [100352, 768], P('dp'), may hold values from -6 to 6
- cotangent: bfloat16 [100352, 768], P('dp'), may hold values from -6 to 6
- skip_mask: int32 [512, 2], P('dp'), may hold values 0 or 1
- pair_index: int32 [512], P('dp'), may hold values from 0 to 511, as said below
- patch_up: bfloat16 [75264], P('dp'), may hold values from -0.4375 to 0.4375
- patch_down: bfloat16 [75264], P('dp'), may hold values from -0.3125 to 0.3125
- channel_up: bfloat16 [2359296], P('dp'), may hold values from -0.21875 to 0.21875
- channel_down: bfloat16 [2359296], P('dp'), may hold values from -0.109375 to 0.109375
- patch_upbias: bfloat16 [384], replicated, may hold values from -3 to 3
- patch_downbias: bfloat16 [196], replicated, may hold values from -3 to 3
- first_gain: bfloat16 [768], P('dp'), may hold values from 0.5 to 1.5
- first_shift: bfloat16 [768], P('dp'), may hold values from -3 to 3
- second_gain: bfloat16 [768], P('dp'), may hold values from 0.5 to 1.5
- second_shift: bfloat16 [768], P('dp'), may hold values from -3 to 3
- channel_upbias: bfloat16 [3072], P('dp'), may hold values from -3 to 3
- channel_downbias: bfloat16 [768], P('dp'), may hold values from -3 to 3
Outputs:
- mixed_out: bfloat16 [100352, 768], P('dp')
- pair_loss: float32 [512], P('dp')
- grad_tokens: float32 [100352, 768], P('dp')
- grad_patch_up: float32 [75264], P('dp')
- grad_patch_down: float32 [75264], P('dp')
- grad_channel_up: float32 [2359296], P('dp')
- grad_channel_down: float32 [2359296], P('dp')
- grad_patch_upbias: float32 [384], replicated
- grad_patch_downbias: float32 [196], replicated
- grad_first_gain: float32 [768], P('dp')
- grad_first_shift: float32 [768], P('dp')
- grad_second_gain: float32 [768], P('dp')
- grad_second_shift: float32 [768], P('dp')
- grad_channel_upbias: float32 [3072], P('dp')
- grad_channel_downbias: float32 [768], P('dp')
The draws below stay inside these ranges and needn't reach their ends.
Inputs may be any that keep to these rules, and one draw needn't show every extreme that they name: pair_index[pair_index[c]] = c and pair_index[c] != c for every crop c.
All inputs are finite; a program needn't handle non-finite values. No bound on the sum of `skip_mask` on one device may be relied on, other than what follows from the above.
Results may differ from the reference program's by a relative error of at most 0.0075.
Values may be sent and summed in bfloat16 or wider, within the bound.
No kernel may reach another device: no remote copies, remote signals or barrier semaphores. Data moves between devices by JAX's collectives and lax.ppermute only.
A program may use at most 320 MiB of HBM per device.

```python
import jax
import jax.numpy as jnp
from jax import lax

D = 768
S = 196
DS = 384
DC = 3072
CROPS = 512
TOKENS = 100352


def draw_pair_index(key, part):
    key = jax.random.fold_in(key, 11)
    order = jax.random.permutation(key, CROPS).astype(jnp.int32)
    partner_slot = jnp.bitwise_xor(jnp.arange(CROPS, dtype=jnp.int32), 1)
    return jnp.zeros((CROPS,), jnp.int32).at[order].set(order[partner_slot])


def with_ends(values, own_key, low, high):
    longest = values.shape.index(max(values.shape))
    spots = []
    for shift in (0, 1):
        where = [jax.random.randint(jax.random.fold_in(own_key, axis), (), 0, length) for axis, length in enumerate(values.shape)]
        where[longest] = (where[longest] + shift) % values.shape[longest]
        spots.append(tuple(where))
    return values.at[spots[0]].set(low).at[spots[1]].set(high)


def shard_levels(key, dims, split, least, high):
    loudness = 1.0
    for position, parts in split:
        heights = jax.random.uniform(jax.random.fold_in(jax.random.fold_in(key, 6), position), (parts,), jnp.float32, least / len(split), high / len(split))
        loudness = loudness * jnp.repeat(jnp.exp(heights), dims[position] // parts).reshape((-1,) + (1,) * (len(dims) - 1 - position))
    return loudness


def normal_values(rng, shape, scale, most, split=(), kind=jnp.bfloat16):
    loudness = shard_levels(rng, shape, split, -0.22, 0.18) if split else 1.0
    array = jax.random.normal(rng, shape, jnp.float32) * scale * loudness
    return jnp.minimum(jnp.maximum(array, -most), most).astype(kind)


def setup_inputs(seed: int = 0) -> dict:
    key_list = jax.random.split(jax.random.key(seed), 17)
    tokens = normal_values(key_list[0], (TOKENS, D), 1.0, 6.0, ((0, 32),))
    cotangent = normal_values(key_list[1], (TOKENS, D), 1.0, 6.0, ((0, 32),))
    skip_mask = with_ends((jax.random.randint(key_list[2], (CROPS, 2), 0, 4) < 3).astype(jnp.int32), jax.random.fold_in(key_list[2], 1), 0, 1)
    pair_index = draw_pair_index(jax.random.fold_in(key_list[16], 71), 0)
    patch_up = normal_values(key_list[4], (S * DS,), S ** -0.5, 0.4375, ((0, 32),))
    patch_down = normal_values(key_list[5], (DS * S,), DS ** -0.5, 0.3125, ((0, 32),))
    channel_up = normal_values(key_list[6], (D * DC,), D ** -0.5, 0.21875, ((0, 32),))
    channel_down = normal_values(key_list[7], (DC * D,), DC ** -0.5, 0.109375, ((0, 32),))
    patch_upbias = normal_values(key_list[8], (DS,), 0.5, 3.0)
    patch_downbias = normal_values(key_list[9], (S,), 0.5, 3.0)
    first_gain = jnp.clip(1.0 + 0.1 * jax.random.normal(key_list[10], (D,), jnp.float32), 0.5, 1.5).astype(jnp.bfloat16)
    first_shift = normal_values(key_list[11], (D,), 0.5, 3.0, ((0, 32),))
    second_gain = jnp.clip(1.0 + 0.1 * jax.random.normal(key_list[12], (D,), jnp.float32), 0.5, 1.5).astype(jnp.bfloat16)
    second_shift = normal_values(key_list[13], (D,), 0.5, 3.0, ((0, 32),))
    channel_upbias = normal_values(key_list[14], (DC,), 0.5, 3.0, ((0, 32),))
    channel_downbias = normal_values(key_list[15], (D,), 0.5, 3.0, ((0, 32),))
    return dict(tokens=tokens, cotangent=cotangent, skip_mask=skip_mask, pair_index=pair_index, patch_up=patch_up, patch_down=patch_down, channel_up=channel_up, channel_down=channel_down, patch_upbias=patch_upbias, patch_downbias=patch_downbias, first_gain=first_gain, first_shift=first_shift, second_gain=second_gain, second_shift=second_shift, channel_upbias=channel_upbias, channel_downbias=channel_downbias)


eps_norm = 1e-06
keep_scale = 4.0 / 3.0
full_precision_mode = lax.Precision.HIGHEST

@jax.custom_vjp
def reduced_precision_cast(v):
    return lax.optimization_barrier(v.astype(jnp.bfloat16)).astype(jnp.float32)

@jax.custom_vjp
def reduced_precision_return(v):
    return v

def low_keep(v):
    return (reduced_precision_cast(v), None)

def low_pass(kept, grad):
    return (grad,)

def back_keep(v):
    return (v, None)

def back_low(kept, grad):
    return (reduced_precision_cast(grad),)
reduced_precision_cast.defvjp(low_keep, low_pass)
reduced_precision_return.defvjp(back_keep, back_low)

def exact_error_linear(values):
    return 0.5 * values * (1.0 + lax.erf(values * 0.7071067811865476))

def layer_norm(values):
    center = values - lax.optimization_barrier(jnp.mean(values, axis=-1, keepdims=True))
    return center * lax.rsqrt(lax.optimization_barrier(jnp.mean(center * center, axis=-1, keepdims=True)) + eps_norm)

def crop_forward(params, patches, scales):
    up_patch, down_patch, up_channel, channel_down_weight, bias_lift, bias_mix, gain_one, shift_one, gain_two, shift_two, bias_channel, output_bias_vector = params
    normed = reduced_precision_cast(layer_norm(patches) * gain_one + shift_one)
    lifted = reduced_precision_return(jnp.dot(normed.T, up_patch, precision=full_precision_mode) + bias_lift)
    active = reduced_precision_cast(exact_error_linear(lifted))
    mixing = reduced_precision_return(jnp.dot(active, down_patch, precision=full_precision_mode) + bias_mix)
    middle = patches + scales[0] * mixing.T
    second = reduced_precision_cast(layer_norm(middle) * gain_two + shift_two)
    hidden_units = reduced_precision_return(jnp.dot(second, up_channel, precision=full_precision_mode) + bias_channel)
    activation_values = reduced_precision_cast(exact_error_linear(hidden_units))
    residual_branch = reduced_precision_return(jnp.dot(activation_values, channel_down_weight, precision=full_precision_mode) + output_bias_vector)
    return middle + scales[1] * residual_branch

def forward(params, crops, scales, pair_index):
    kept_fn = jax.checkpoint(crop_forward)

    def one_crop(element):
        return kept_fn(params, element[0], element[1])
    outputs = lax.map(one_crop, (crops, scales))
    pooled = lax.optimization_barrier(jnp.mean(outputs, axis=1))
    differ = pooled - jnp.take(pooled, pair_index, axis=0)
    return (outputs, 2.0 * lax.optimization_barrier(jnp.sum(differ * differ, axis=1)))

def reference(tokens, cotangent, skip_mask, pair_index, patch_up, patch_down, channel_up, channel_down, patch_upbias, patch_downbias, first_gain, first_shift, second_gain, second_shift, channel_upbias, channel_downbias):
    single_float = jnp.float32
    crops = tokens.astype(single_float).reshape(CROPS, S, D)
    upstream = cotangent.astype(single_float).reshape(CROPS, S, D)
    scales = skip_mask.astype(single_float) * keep_scale
    params = (patch_up.astype(single_float).reshape(S, DS), patch_down.astype(single_float).reshape(DS, S), channel_up.astype(single_float).reshape(D, DC), channel_down.astype(single_float).reshape(DC, D), patch_upbias.astype(single_float), patch_downbias.astype(single_float), first_gain.astype(single_float), first_shift.astype(single_float), second_gain.astype(single_float), second_shift.astype(single_float), channel_upbias.astype(single_float), channel_downbias.astype(single_float))

    def objective(weights, inputs):
        return forward(weights, inputs, scales, pair_index)
    (outputs, losses), pull = jax.vjp(objective, params, crops)
    weight_grads, input_grad = pull((upstream, jnp.ones((CROPS,), single_float)))
    return (outputs.reshape(TOKENS, D).astype(jnp.bfloat16), losses, input_grad.reshape(TOKENS, D), weight_grads[0].reshape(S * DS), weight_grads[1].reshape(DS * S), weight_grads[2].reshape(D * DC), weight_grads[3].reshape(DC * D), weight_grads[4], weight_grads[5], weight_grads[6], weight_grads[7], weight_grads[8], weight_grads[9], weight_grads[10], weight_grads[11])
```

```python
import functools

import jax
import jax.numpy as jnp
import numpy as np
from jax import lax
from jax.experimental import pallas as pl
from jax.experimental.pallas import tpu as pltpu
from jax.sharding import PartitionSpec as P

D = 768
S = 196
DS = 384
DC = 3072
HALF = DC // 2

GROUP = 4
TILE = GROUP * S
WIN = 208
STEP = 192
ONES = 16

eps_norm = 1e-06
keep_scale = 4.0 / 3.0
f32 = jnp.float32
bf16 = jnp.bfloat16
VMEM = 60 * 1024 * 1024


def params(limit=VMEM):
    return pltpu.CompilerParams(vmem_limit_bytes=limit)


def resident(shape):
    zeros = (0,) * len(shape)
    return pl.BlockSpec(shape, lambda *_: zeros, pipeline_mode=pl.Buffered(1))


def smem():
    return pl.BlockSpec(memory_space=pltpu.SMEM)


def dot(a, b):
    return jnp.dot(a, b, preferred_element_type=f32)


def dot_nt(a, b):
    return lax.dot_general(a, b, (((1,), (1,)), ((), ())), preferred_element_type=f32)


def gelu_and_slope(z):
    phi = 0.5 * (1.0 + lax.erf(z * 0.7071067811865476))
    return z * phi, phi + z * jnp.exp(-0.5 * z * z) * 0.3989422804014327


def normalize(v):
    center = v - jnp.mean(v, axis=-1, keepdims=True)
    inv = lax.rsqrt(jnp.mean(center * center, axis=-1, keepdims=True) + eps_norm)
    return center * inv, inv


def per_row(values, shape, start=0):
    rows = lax.broadcasted_iota(jnp.int32, shape, 0) + start
    out = jnp.broadcast_to(values[GROUP - 1], shape)
    for c in range(GROUP - 2, -1, -1):
        out = jnp.where(rows < (c + 1) * S, values[c], out)
    return out


def crop_sum(read, c):
    lo, hi = c * S, (c + 1) * S
    base = c * STEP
    width = read(base, 8).shape[1]
    total = jnp.sum(read(base + 16, STEP - 16), axis=0, keepdims=True)
    for piece in (base, base + STEP):
        rows = lax.broadcasted_iota(jnp.int32, (16, width), 0) + piece
        ok = (rows >= lo) & (rows < hi)
        total += jnp.sum(jnp.where(ok, read(piece, 16), 0.0), axis=0, keepdims=True)
    return total


def token_forward_kernel(keep, x, wut, wdt, bu, bd, g1, s1, g2, s2, x1, h2, act, slope, sums, h1):
    i = pl.program_id(0)
    tokens = x[...].astype(f32)
    normed, _ = normalize(tokens)
    h1[...] = (normed * g1[...] + s1[...]).astype(bf16)
    x1[...] = tokens
    for c in range(GROUP):
        lifted = dot(wut[c], h1[pl.ds(c * STEP, WIN), :]) + bu[...]
        value, grad = gelu_and_slope(lifted)
        value = value.astype(bf16)
        act[c] = value
        slope[c] = grad.astype(bf16)
        mixed = dot(wdt[c], value) + bd[c]
        x1[pl.ds(c * STEP, WIN), :] += keep[i * GROUP + c, 0] * mixed
    normed, _ = normalize(x1[...])
    h2[...] = (normed * g2[...] + s2[...]).astype(bf16)
    for c in range(GROUP):
        sums[0, pl.ds(c, 1), :] = crop_sum(lambda a, n: x1[pl.ds(a, n), :], c)


def token_forward(keep, x, wut, wdt, bu, bd, g1, s1, g2, s2):
    rows = x.shape[0]
    crops = rows // S
    grid = rows // TILE
    tile = pl.BlockSpec((TILE, D), lambda i: (i, 0))
    hidden = pl.BlockSpec((GROUP, DS, D), lambda i: (i, 0, 0))
    vec = resident((1, D))
    return pl.pallas_call(
        token_forward_kernel,
        grid=(grid,),
        in_specs=[
            smem(),
            tile,
            resident((GROUP, DS, WIN)),
            resident((GROUP, WIN, DS)),
            resident((DS, 1)),
            resident((GROUP, WIN, 1)),
            vec,
            vec,
            vec,
            vec,
        ],
        out_specs=[tile, tile, hidden, hidden, pl.BlockSpec((1, GROUP, D), lambda i: (i, 0, 0))],
        out_shape=[
            jax.ShapeDtypeStruct((rows, D), f32),
            jax.ShapeDtypeStruct((rows, D), bf16),
            jax.ShapeDtypeStruct((crops, DS, D), bf16),
            jax.ShapeDtypeStruct((crops, DS, D), bf16),
            jax.ShapeDtypeStruct((grid, GROUP, D), f32),
        ],
        scratch_shapes=[pltpu.VMEM((TILE, D), bf16)],
        compiler_params=params(),
        cost_estimate=pl.CostEstimate(
            flops=4 * rows * DS * D, bytes_accessed=rows * D * 12, transcendentals=0
        ),
        name="token_forward",
    )(keep, x, wut, wdt, bu, bd, g1, s1, g2, s2)


def hidden_kernel(h2, w, bias, members, act, slope, sums):
    chunk = 512
    for j in range(DC // chunk):
        cols = pl.ds(j * chunk, chunk)
        z = dot(h2[...], w[:, cols]) + bias[:, cols]
        value, grad = gelu_and_slope(z)
        value = value.astype(bf16)
        act[:, cols] = value
        slope[:, cols] = grad.astype(bf16)
        sums[0, :, cols] = dot(members[...], value)


def hidden_forward(h2, w, bias, members):
    rows = h2.shape[0]
    grid = rows // TILE
    wide = pl.BlockSpec((TILE, DC), lambda i: (i, 0))
    return pl.pallas_call(
        hidden_kernel,
        grid=(grid,),
        in_specs=[
            pl.BlockSpec((TILE, D), lambda i: (i, 0)),
            resident((D, DC)),
            resident((1, DC)),
            resident((16, TILE)),
        ],
        out_specs=[wide, wide, pl.BlockSpec((1, 16, DC), lambda i: (i, 0, 0))],
        out_shape=[
            jax.ShapeDtypeStruct((rows, DC), bf16),
            jax.ShapeDtypeStruct((rows, DC), bf16),
            jax.ShapeDtypeStruct((grid, 16, DC), f32),
        ],
        compiler_params=params(),
        cost_estimate=pl.CostEstimate(
            flops=3 * rows * D * DC, bytes_accessed=rows * DC * 4, transcendentals=0
        ),
        name="hidden_forward",
    )(h2, w, bias, members)


def pooled_kernel(sums, w, x_sums, scale, bias, out, sent):
    k = pl.program_id(0)
    part = sums[...]
    high = part.astype(bf16)
    low = (part - high.astype(f32)).astype(bf16)
    total = dot(high, w[...]) + dot(low, w[...])

    @pl.when(k == 0)
    def _():
        out[...] = total

    @pl.when(k > 0)
    def _():
        out[...] += total

    @pl.when(k == pl.num_programs(0) - 1)
    def _():
        pooled = (x_sums[...] + scale[...] * (out[...] + S * bias[...])) * (1.0 / S)
        out[...] = pooled
        sent[...] = pooled.astype(bf16)


def pooled_output(sums, w, x_sums, scale, bias):
    crops = sums.shape[0]
    block = 1024
    return pl.pallas_call(
        pooled_kernel,
        grid=(DC // block,),
        in_specs=[
            pl.BlockSpec((crops, block), lambda k: (0, k)),
            pl.BlockSpec((block, D), lambda k: (k, 0)),
            resident((crops, D)),
            resident((crops, 1)),
            resident((1, D)),
        ],
        out_specs=[pl.BlockSpec((crops, D), lambda k: (0, 0))] * 2,
        out_shape=[jax.ShapeDtypeStruct((crops, D), f32), jax.ShapeDtypeStruct((crops, D), bf16)],
        compiler_params=params(),
        name="pooled_output",
    )(sums, w, x_sums, scale, bias)


def output_kernel(keep, act, w, x1, bias, out):
    i = pl.program_id(0)
    scale = per_row([keep[i * GROUP + c, 1] for c in range(GROUP)], (TILE, 1))
    branch = dot(act[...], w[...]) + bias[...]
    out[...] = (x1[...] + scale * branch).astype(bf16)


def output_forward(keep, act, w, x1, bias):
    rows = x1.shape[0]
    tile = pl.BlockSpec((TILE, D), lambda i: (i, 0))
    return pl.pallas_call(
        output_kernel,
        grid=(rows // TILE,),
        in_specs=[
            smem(),
            pl.BlockSpec((TILE, DC), lambda i: (i, 0)),
            resident((DC, D)),
            tile,
            resident((1, D)),
        ],
        out_specs=tile,
        out_shape=jax.ShapeDtypeStruct((rows, D), bf16),
        compiler_params=params(),
        cost_estimate=pl.CostEstimate(
            flops=2 * rows * D * DC, bytes_accessed=rows * DC * 2 + rows * D * 6, transcendentals=0
        ),
        name="output_forward",
    )(keep, act, w, x1, bias)


def residual_kernel(keep, cotangent, differ, out, sums):
    i = pl.program_id(0)
    scale = per_row([keep[i * GROUP + c, 1] for c in range(GROUP)], (TILE, 1))
    shift = per_row([differ[0, pl.ds(c, 1), :] for c in range(GROUP)], (TILE, D))
    grad = (scale * (cotangent[...].astype(f32) + (8.0 / S) * shift)).astype(bf16)
    out[...] = grad
    total = jnp.sum(grad.astype(f32), axis=0, keepdims=True)

    @pl.when(i == 0)
    def _():
        sums[...] = total

    @pl.when(i > 0)
    def _():
        sums[...] += total


def residual_gradient(keep, cotangent, differ):
    rows = cotangent.shape[0]
    tile = pl.BlockSpec((TILE, D), lambda i: (i, 0))
    return pl.pallas_call(
        residual_kernel,
        grid=(rows // TILE,),
        in_specs=[smem(), tile, pl.BlockSpec((1, GROUP, D), lambda i: (i, 0, 0))],
        out_specs=[tile, pl.BlockSpec((1, D), lambda i: (0, 0))],
        out_shape=[jax.ShapeDtypeStruct((rows, D), bf16), jax.ShapeDtypeStruct((1, D), f32)],
        compiler_params=params(),
        name="residual_gradient",
    )(keep, cotangent, differ)


def hidden_backward_kernel(grad, h2t, w, slope, gz, dw, db):
    part = dot_nt(grad[...], w[...]) * slope[...].astype(f32)
    db[...] = jnp.sum(part, axis=0, keepdims=True)
    gz[...] = part.astype(bf16)
    dw[0] = dot(h2t[...], gz[...]).astype(bf16)


def hidden_backward(grad, h2t, w, slope):
    rows = grad.shape[0]
    chunk = 384
    per = D // chunk
    return pl.pallas_call(
        hidden_backward_kernel,
        grid=(DC // chunk,),
        in_specs=[
            resident((rows, D)),
            resident((D, rows)),
            pl.BlockSpec((chunk, D), lambda j: (j, 0)),
            pl.BlockSpec((rows, chunk), lambda j: (0, j)),
        ],
        out_specs=[
            pl.BlockSpec((rows, chunk), lambda j: (0, j)),
            pl.BlockSpec((1, D, chunk), lambda j: (j // per, 0, j % per)),
            pl.BlockSpec((1, chunk), lambda j: (0, j)),
        ],
        out_shape=[
            jax.ShapeDtypeStruct((rows, DC), bf16),
            jax.ShapeDtypeStruct((DC // D, D, D), bf16),
            jax.ShapeDtypeStruct((1, DC), f32),
        ],
        compiler_params=params(),
        cost_estimate=pl.CostEstimate(
            flops=4 * rows * D * DC, bytes_accessed=rows * DC * 4, transcendentals=0
        ),
        name="hidden_backward",
    )(grad, h2t, w, slope)


def token_backward_kernel(
    keep, gz, w, x1, cotangent, differ, x, act, slope, wd, wu, g1, s1, g2,
    out, dwd, dwu, vecs, gx1, gv, h1, gh1,
):
    i = pl.program_id(0)

    @pl.when(i == 0)
    def _():
        dwd[...] = jnp.zeros_like(dwd)
        dwu[...] = jnp.zeros_like(dwu)
        vecs[...] = jnp.zeros_like(vecs)

    def norm_back(grad, gain, normed, inv):
        scaled = grad * gain
        return inv * (
            scaled
            - jnp.mean(scaled, axis=-1, keepdims=True)
            - normed * jnp.mean(scaled * normed, axis=-1, keepdims=True)
        )

    def add_vec(row, value):
        vecs[pl.ds(row, 1), :] += jnp.sum(value, axis=0, keepdims=True)

    gh2 = dot_nt(gz[...], w[...])
    normed, inv = normalize(x1[...])
    add_vec(0, gh2 * normed)
    add_vec(1, gh2)
    shift = per_row([differ[0, pl.ds(c, 1), :] for c in range(GROUP)], (TILE, D))
    gx1[...] = (
        cotangent[...].astype(f32)
        + (8.0 / S) * shift
        + norm_back(gh2, g2[...], normed, inv)
    )
    scale = per_row([keep[i * GROUP + c, 0] for c in range(GROUP)], (TILE, 1))
    gv[...] = (scale * gx1[...]).astype(bf16)

    normed, inv = normalize(x[...].astype(f32))
    h1[...] = (normed * g1[...] + s1[...]).astype(bf16)
    gh1[...] = jnp.zeros_like(gh1)
    ones = jnp.ones((ONES, D), bf16)
    for c in range(GROUP):
        rows = pl.ds(c * STEP, WIN)
        piece = gv[rows, :]
        dwd[c] += dot_nt(jnp.concatenate([act[c], ones], axis=0), piece)
        gu = (dot(wd[c], piece) * slope[c].astype(f32)).astype(bf16)
        dwu[c] += dot_nt(jnp.concatenate([h1[rows, :], ones], axis=0), gu)
        gh1[rows, :] += dot(wu[c], gu)
    add_vec(2, gh1[...] * normed)
    add_vec(3, gh1[...])
    out[...] = gx1[...] + norm_back(gh1[...], g1[...], normed, inv)


def token_backward(keep, gz, w, x1, cotangent, differ, x, act, slope, wd, wu, g1, s1, g2):
    rows = x.shape[0]
    tile = pl.BlockSpec((TILE, D), lambda i: (i, 0))
    hidden = pl.BlockSpec((GROUP, DS, D), lambda i: (i, 0, 0))
    vec = resident((1, D))
    return pl.pallas_call(
        token_backward_kernel,
        grid=(rows // TILE,),
        in_specs=[
            smem(),
            pl.BlockSpec((TILE, DC), lambda i: (i, 0)),
            resident((D, DC)),
            tile,
            tile,
            pl.BlockSpec((1, GROUP, D), lambda i: (i, 0, 0)),
            tile,
            hidden,
            hidden,
            resident((GROUP, DS, WIN)),
            resident((GROUP, WIN, DS)),
            vec,
            vec,
            vec,
        ],
        out_specs=[
            tile,
            pl.BlockSpec((GROUP, DS + ONES, WIN), lambda i: (0, 0, 0)),
            pl.BlockSpec((GROUP, WIN + ONES, DS), lambda i: (0, 0, 0)),
            pl.BlockSpec((8, D), lambda i: (0, 0)),
        ],
        out_shape=[
            jax.ShapeDtypeStruct((rows, D), f32),
            jax.ShapeDtypeStruct((GROUP, DS + ONES, WIN), f32),
            jax.ShapeDtypeStruct((GROUP, WIN + ONES, DS), f32),
            jax.ShapeDtypeStruct((8, D), f32),
        ],
        scratch_shapes=[
            pltpu.VMEM((TILE, D), f32),
            pltpu.VMEM((TILE, D), bf16),
            pltpu.VMEM((TILE, D), bf16),
            pltpu.VMEM((TILE, D), f32),
        ],
        compiler_params=params(),
        cost_estimate=pl.CostEstimate(
            flops=2 * rows * D * DC + 10 * rows * DS * D,
            bytes_accessed=rows * DC * 2 + rows * D * 16,
            transcendentals=0,
        ),
        name="token_backward",
    )(keep, gz, w, x1, cotangent, differ, x, act, slope, wd, wu, g1, s1, g2)


class Net:
    def __init__(self, n):
        chips = n // 2
        side = 1
        while 2 * side * side * side < chips:
            side *= 2
        if 2 * side * side * side != chips:
            raise ValueError("unknown slice")
        self.n, self.side = n, side
        self.core = [1]
        self.x = [2 * k for k in range(1, side)]
        self.y = [2 * side * k for k in range(1, side)]
        self.z = [2 * side * side * k for k in range(1, 2 * side)]
        self.xy = [2 * k for k in range(1, side * side)]
        self.me = lax.axis_index("dp")
        self.at_core = self.me % 2
        self.at_x = (self.me // 2) % side
        self.at_y = (self.me // (2 * side)) % side
        self.at_z = self.me // (2 * side * side)

    def swap(self, value, offset):
        return lax.ppermute(value, "dp", [(i, i ^ offset) for i in range(self.n)])

    def spread(self, value, offsets):
        return jnp.stack([value] + [self.swap(value, o) for o in offsets])

    def gather_small(self, value):
        held = value
        order = np.zeros((1,), np.int64)
        for offsets in (self.z, self.xy, self.core):
            held = self.spread(held, offsets)
            order = (np.array([0] + offsets)[:, None] + order[None, :]).reshape(-1)
        held = held.reshape(self.n, -1)
        pick = (jnp.arange(self.n)[:, None] ^ self.me) == jnp.asarray(order, jnp.int32)[None, :]
        return dot(pick.astype(bf16), held).astype(bf16)

    def gather_parts(self, value):
        rows, _, cols = value.shape
        kz, k = 2 * self.side, self.side
        held = self.spread(value, self.z)
        order_z = jnp.arange(kz) ^ self.at_z
        order_x = jnp.arange(k) ^ self.at_x
        order_y = jnp.arange(k) ^ self.at_y
        first = self.spread(self.spread(held[:, :, 0], self.y), self.x)
        second = self.spread(self.spread(held[:, :, 1], self.x), self.y)
        first = first.transpose(2, 1, 0, 3, 4)
        second = second.transpose(2, 0, 1, 3, 4)
        both = jnp.concatenate([first, second], axis=-1)
        both = jnp.take(both, order_z, axis=0)
        both = jnp.take(both, order_y, axis=1)
        both = jnp.take(both, order_x, axis=2)
        return both.reshape(kz * k * k * rows, 2 * cols)

    def pick(self, value, index, axis):
        return lax.dynamic_index_in_dim(value, index, axis, keepdims=False)

    def reduce_axis(self, value, axis, at, offsets, unit):
        total = self.pick(value, at, axis)
        for k, offset in enumerate(offsets):
            part = self.pick(value, at ^ (k + 1), axis).astype(bf16)
            total = total + self.swap(part, offset).astype(f32)
        return total

    def scatter_part(self, value, x_first):
        if x_first:
            value = self.reduce_axis(value, 2, self.at_x, self.x, 2)
            value = self.reduce_axis(value, 1, self.at_y, self.y, 2)
        else:
            value = self.reduce_axis(value, 1, self.at_y, self.y, 2)
            value = self.reduce_axis(value, 1, self.at_x, self.x, 2)
        return self.reduce_axis(value, 0, self.at_z, self.z, 2)

    def scatter_chips(self, value):
        kz, k = 2 * self.side, self.side
        value = value.reshape((kz, k, k) + value.shape[1:])
        return jnp.stack(
            [self.scatter_part(value[:, :, :, :, 0], True), self.scatter_part(value[:, :, :, :, 1], False)],
            axis=1,
        )

    def scatter_small(self, value):
        kz, k = 2 * self.side, self.side
        value = value.reshape(kz, k * k, 2, -1)
        value = self.reduce_axis(value, 2, self.at_core, self.core, 1)
        value = self.reduce_axis(value, 1, (self.me // 2) % (k * k), self.xy, 2)
        return self.reduce_axis(value, 0, self.at_z, self.z, 2)

    def sum_all(self, value):
        for bit in range(self.n.bit_length() - 1):
            value = value + self.swap(value, 1 << bit)
        return value


def shifted(matrix, axis):
    out = []
    for c in range(GROUP):
        pads = [(0, 0)] * matrix.ndim
        pads[axis] = (4 * c, WIN - S - 4 * c)
        out.append(jnp.pad(matrix, pads))
    return jnp.stack(out)


def by_core(at_core, value):
    return jnp.where(at_core == 0, value, value[::-1])


def per_device(
    tokens,
    cotangent,
    skip_mask,
    pair_index,
    patch_up,
    patch_down,
    channel_up,
    channel_down,
    patch_upbias,
    patch_downbias,
    first_gain,
    first_shift,
    second_gain,
    second_shift,
    channel_upbias,
    channel_downbias,
    devices,
):
    net = Net(devices)
    chips = devices // 2
    core = net.at_core
    rows = tokens.shape[0]
    crops = rows // S
    unit_d = D // devices
    unit_h = DC // devices

    small = [
        patch_up, patch_down, first_gain, first_shift, second_gain, second_shift, channel_upbias, channel_downbias,
    ]
    sizes = [v.shape[0] for v in small]
    length = sum(sizes)
    padded = -(-length // 1024) * 1024
    packed = jnp.pad(jnp.concatenate(small), (0, padded - length))
    every = net.gather_small(packed)
    pieces, start = [], 0
    for size in sizes:
        pieces.append(every[:, start : start + size].reshape(-1))
        start += size
    up, down = pieces[0].reshape(S, DS), pieces[1].reshape(DS, S)
    g1, s1, g2, s2 = [v.astype(f32).reshape(1, D) for v in pieces[2:6]]
    bias_hidden = by_core(core, pieces[6].reshape(chips, 2, unit_h).transpose(1, 0, 2)).reshape(1, DC).astype(f32)
    bias_out = pieces[7].reshape(1, D).astype(f32)

    shard = channel_up.reshape(unit_d, chips, 2, unit_h).transpose(2, 0, 1, 3).reshape(2, unit_d, HALF)
    shard = by_core(core, shard)
    other = net.swap(shard[1], 1)
    mine = by_core(core, jnp.stack([shard[0], other]))
    mine_up = net.gather_parts(mine.reshape(2 * unit_d, 2, HALF // 2))
    w_up = jnp.concatenate([mine_up, net.swap(mine_up, 1)], axis=1)
    mine_down = net.gather_parts(channel_down.reshape(unit_h, 2, D // 2))
    w_down = jnp.concatenate([mine_down, net.swap(mine_down, 1)], axis=0)

    keep = skip_mask.astype(f32) * keep_scale
    up_pad = shifted(up, 0)
    down_pad = shifted(down, 1)
    bias_mix = shifted(patch_downbias.astype(f32).reshape(S, 1), 0)
    x1, h2, act_t, slope_t, x_sums = token_forward(
        keep,
        tokens,
        up_pad.transpose(0, 2, 1),
        down_pad.transpose(0, 2, 1),
        patch_upbias.astype(f32).reshape(DS, 1),
        bias_mix,
        g1,
        s1,
        g2,
        s2,
    )
    members = np.zeros((16, TILE), np.float32)
    for c in range(GROUP):
        members[c, c * S : (c + 1) * S] = 1.0
    act, slope, act_sums = hidden_forward(h2, w_up, bias_hidden, jnp.asarray(members, bf16))
    pooled, sent = pooled_output(
        act_sums[:, :GROUP].reshape(crops, DC), w_down, x_sums.reshape(crops, D), keep[:, 1:2], bias_out
    )
    everyone = net.gather_small(sent.reshape(-1)).reshape(-1, D)
    outputs = output_forward(keep, act, w_down, x1, bias_out)
    chosen = (pair_index[:, None] == jnp.arange(everyone.shape[0])[None, :]).astype(bf16)
    differ = pooled - dot(chosen, everyone)
    losses = 2.0 * jnp.sum(differ * differ, axis=1)
    differ = differ.reshape(crops // GROUP, GROUP, D)

    grad, grad_bias_out = residual_gradient(keep, cotangent, differ)
    grad_down = lax.dot_general(act, grad, (((0,), (0,)), ((), ())), preferred_element_type=f32).astype(bf16)
    gz, grad_up, grad_bias_hidden = hidden_backward(grad, h2.T, w_down, slope)

    down_other = net.swap(grad_down[HALF:], 1)
    down_sum = (grad_down[:HALF].astype(f32) + down_other.astype(f32)).reshape(chips, unit_h, 2, D // 2)
    down_grad = net.scatter_chips(down_sum).reshape(-1)

    up_other = net.swap(grad_up[2:], 1)
    up_sum = grad_up[:2].astype(f32) + up_other.astype(f32)
    up_sum = up_sum.reshape(2, chips, 2 * unit_d, D).transpose(1, 2, 0, 3)
    up_chip = net.scatter_chips(up_sum).reshape(2, unit_d, HALF)
    up_chip = by_core(core, up_chip)
    up_rows = jnp.stack([up_chip[0], net.swap(up_chip[1], 1)])
    up_rows = by_core(core, up_rows)
    up_grad = up_rows.reshape(2, unit_d, chips, unit_h).transpose(1, 2, 0, 3).reshape(-1)

    grad_tokens, dwd, dwu, vecs = token_backward(
        keep, gz, w_up, x1, cotangent, differ, tokens, act_t, slope_t, down_pad, up_pad, g1, s1, g2
    )
    grad_patch_up = sum(dwu[c, 4 * c : 4 * c + S] for c in range(GROUP))
    grad_patch_down = sum(dwd[c, :DS, 4 * c : 4 * c + S] for c in range(GROUP))
    bias_up = sum(dwu[c, WIN] for c in range(GROUP))
    bias_down = sum(dwd[c, DS, 4 * c : 4 * c + S] for c in range(GROUP))
    bias_hidden_grad = by_core(core, grad_bias_hidden.reshape(2, chips, unit_h)).transpose(1, 0, 2)
    scattered = [
        grad_patch_up, grad_patch_down, vecs[2], vecs[3], vecs[0], vecs[1], bias_hidden_grad, grad_bias_out,
    ]
    scattered = jnp.concatenate([v.reshape(devices, -1) for v in scattered], axis=1)
    scattered = jnp.pad(scattered, ((0, 0), (0, padded - length)))
    own = net.scatter_small(scattered)
    grads, start = [], 0
    for size in sizes:
        grads.append(own[start : start + size])
        start += size
    biases = net.sum_all(jnp.pad(jnp.concatenate([bias_up, bias_down]), (0, 1024 - DS - S)))
    return (
        outputs,
        losses,
        grad_tokens,
        grads[0],
        grads[1],
        up_grad,
        down_grad,
        biases[:DS],
        biases[DS : DS + S],
        grads[2],
        grads[3],
        grads[4],
        grads[5],
        grads[6],
        grads[7],
    )


def solution(mesh):
    row, flat, whole = P("dp", None), P("dp"), P()
    return jax.shard_map(
        functools.partial(per_device, devices=mesh.shape["dp"]),
        mesh=mesh,
        in_specs=(row, row, row, flat, flat, flat, flat, flat, whole, whole) + (flat,) * 6,
        out_specs=(row, flat, row, flat, flat, flat, flat, whole, whole) + (flat,) * 6,
        check_vma=False,
    )
```

```python
import functools

import jax
import jax.numpy as jnp
import numpy as np
from jax import lax
from jax.experimental import pallas as pl
from jax.experimental.pallas import tpu as pltpu
from jax.sharding import PartitionSpec as P

D = 768
S = 196
DS = 384
DC = 3072

GROUP = 4
TILE = GROUP * S
WIN = 208
STEP = 192
ONES = 16

eps_norm = 1e-06
keep_scale = 4.0 / 3.0
f32 = jnp.float32
bf16 = jnp.bfloat16
MIB = 1024 * 1024


def resident(shape):
    zeros = (0,) * len(shape)
    return pl.BlockSpec(shape, lambda *_: zeros, pipeline_mode=pl.Buffered(1))


def smem():
    return pl.BlockSpec(memory_space=pltpu.SMEM)


def anywhere():
    return pl.BlockSpec(memory_space=pl.ANY)


def call(kernel, after, in_specs, args, vmem, **rest):
    count = len(args)

    def body(*refs):
        kernel(*refs[:count], *refs[count + len(after) :])

    return pl.pallas_call(
        body,
        in_specs=list(in_specs) + [anywhere()] * len(after),
        compiler_params=pltpu.CompilerParams(vmem_limit_bytes=vmem * MIB),
        **rest,
    )(*args, *after)


def kept(skip, crop, branch):
    return skip[crop, branch].astype(f32) * keep_scale


def dot(a, b):
    return jnp.dot(a, b, preferred_element_type=f32)


def dot_nt(a, b):
    return lax.dot_general(a, b, (((1,), (1,)), ((), ())), preferred_element_type=f32)


def gelu_and_slope(z):
    phi = 0.5 * (1.0 + lax.erf(z * 0.7071067811865476))
    return z * phi, phi + z * jnp.exp(-0.5 * z * z) * 0.3989422804014327


def normalize(v):
    center = v - jnp.mean(v, axis=-1, keepdims=True)
    inv = lax.rsqrt(jnp.mean(center * center, axis=-1, keepdims=True) + eps_norm)
    return center * inv, inv


def join(values, axis, total):
    out, start = None, 0
    for v in values:
        pads = [(0, 0)] * v.ndim
        pads[axis] = (start, total - start - v.shape[axis])
        start += v.shape[axis]
        v = jnp.pad(v, pads)
        out = v if out is None else out + v
    return out


def per_row(values, shape, start=0):
    rows = lax.broadcasted_iota(jnp.int32, shape, 0) + start
    out = jnp.broadcast_to(values[GROUP - 1], shape)
    for c in range(GROUP - 2, -1, -1):
        out = jnp.where(rows < (c + 1) * S, values[c], out)
    return out


def crop_sum(read, c):
    lo, hi = c * S, (c + 1) * S
    base = c * STEP
    width = read(base, 8).shape[1]
    total = jnp.sum(read(base + 16, STEP - 16), axis=0, keepdims=True)
    for piece in (base, base + STEP):
        rows = lax.broadcasted_iota(jnp.int32, (16, width), 0) + piece
        ok = (rows >= lo) & (rows < hi)
        total += jnp.sum(jnp.where(ok, read(piece, 16), 0.0), axis=0, keepdims=True)
    return total


def token_forward_kernel(skip, x, wut, wdt, bu, bd, vecs, x1, h2, act, slope, h1):
    i = pl.program_id(0)
    tokens = x[...].astype(f32)
    normed, _ = normalize(tokens)
    h1[...] = (normed * vecs[0:1, :] + vecs[1:2, :]).astype(bf16)
    x1[...] = tokens
    for c in range(GROUP):
        lifted = dot(wut[c], h1[pl.ds(c * STEP, WIN), :]) + bu[...]
        value, grad = gelu_and_slope(lifted)
        value = value.astype(bf16)
        act[c] = value
        slope[c] = grad.astype(bf16)
        mixed = dot(wdt[c], value) + bd[c]
        x1[pl.ds(c * STEP, WIN), :] += kept(skip, i * GROUP + c, 0) * mixed
    normed, _ = normalize(x1[...])
    h2[...] = (normed * vecs[2:3, :] + vecs[3:4, :]).astype(bf16)


def token_forward(skip, x, wut, wdt, bu, bd, vecs, after=()):
    rows = x.shape[0]
    crops = rows // S
    tile = pl.BlockSpec((TILE, D), lambda i: (i, 0))
    hidden = pl.BlockSpec((GROUP, DS, D), lambda i: (i, 0, 0))
    return call(
        token_forward_kernel,
        after,
        [
            smem(),
            tile,
            resident((GROUP, DS, WIN)),
            resident((GROUP, WIN, DS)),
            resident((DS, 1)),
            resident((GROUP, WIN, 1)),
            resident((4, D)),
        ],
        (skip, x, wut, wdt, bu, bd, vecs),
        vmem=40,
        grid=(rows // TILE,),
        out_specs=[tile, tile, hidden, hidden],
        out_shape=[
            jax.ShapeDtypeStruct((rows, D), f32),
            jax.ShapeDtypeStruct((rows, D), bf16),
            jax.ShapeDtypeStruct((crops, DS, D), bf16),
            jax.ShapeDtypeStruct((crops, DS, D), bf16),
        ],
        scratch_shapes=[pltpu.VMEM((TILE, D), bf16)],
        cost_estimate=pl.CostEstimate(
            flops=20 * rows * DS * D, bytes_accessed=rows * D * 12, transcendentals=0
        ),
        name="token_forward",
    )


def channel_forward_kernel(
    skip, h2, up, down, x1, bias_hidden, bias_out, cotangent, out, scaled, act_low, act_high, z_out, sums, pooled
):
    i = pl.program_id(0)
    chunk = 512
    count = DC // chunk
    branch = jnp.broadcast_to(bias_out[...], (TILE, D))

    def hidden(j):
        cols = pl.ds(j * chunk, chunk)
        return dot(h2[...], up[:, cols]) + bias_hidden[:, cols]

    z = hidden(0)
    for j in range(count):
        cols = pl.ds(j * chunk, chunk)
        later = hidden(j + 1) if j + 1 < count else None
        z_out[:, cols] = z.astype(bf16)
        value = z * (0.5 * (1.0 + lax.erf(z * 0.7071067811865476)))
        for c in range(GROUP):
            sums[0, pl.ds(c, 1), cols] = crop_sum(lambda a, n: value[a : a + n], c)
        value = value.astype(bf16)
        half, k = divmod(j, count // 2)
        (act_low, act_high)[half][:, pl.ds(k * chunk, chunk)] = value
        branch += dot(value, down[cols, :])
        z = later
    scale = per_row([kept(skip, i * GROUP + c, 1) for c in range(GROUP)], (TILE, 1))
    y = x1[...] + scale * branch
    out[...] = y.astype(bf16)
    scaled[...] = (scale * cotangent[...].astype(f32)).astype(bf16)
    for c in range(GROUP):
        pooled[0, pl.ds(c, 1), :] = crop_sum(lambda a, n: y[a : a + n], c) * (1.0 / S)


def channel_forward(skip, h2, up, down, x1, bias_hidden, bias_out, cotangent, after=()):
    rows = x1.shape[0]
    grid = rows // TILE
    tile = pl.BlockSpec((TILE, D), lambda i: (i, 0))
    half = pl.BlockSpec((TILE, DC // 2), lambda i: (i, 0))
    return call(
        channel_forward_kernel,
        after,
        [
            smem(),
            tile,
            resident((D, DC)),
            resident((DC, D)),
            tile,
            resident((1, DC)),
            resident((1, D)),
            tile,
        ],
        (skip, h2, up, down, x1, bias_hidden, bias_out, cotangent),
        vmem=60,
        grid=(grid,),
        out_specs=[
            tile,
            tile,
            half,
            half,
            pl.BlockSpec((TILE, DC), lambda i: (i, 0)),
            pl.BlockSpec((1, GROUP, DC), lambda i: (i, 0, 0)),
            pl.BlockSpec((1, GROUP, D), lambda i: (i, 0, 0)),
        ],
        out_shape=[
            jax.ShapeDtypeStruct((rows, D), bf16),
            jax.ShapeDtypeStruct((rows, D), bf16),
            jax.ShapeDtypeStruct((rows, DC // 2), bf16),
            jax.ShapeDtypeStruct((rows, DC // 2), bf16),
            jax.ShapeDtypeStruct((rows, DC), bf16),
            jax.ShapeDtypeStruct((grid, GROUP, DC), f32),
            jax.ShapeDtypeStruct((grid, GROUP, D), f32),
        ],
        cost_estimate=pl.CostEstimate(
            flops=4 * rows * D * DC, bytes_accessed=rows * DC * 4 + rows * D * 10, transcendentals=0
        ),
        name="channel_forward",
    )


def lane_blocks(rows):
    count = max(rows // 768, 1)
    return [(k * 768, 768 if k < count - 1 else rows - 768 * (count - 1)) for k in range(count)]


def hidden_backward_kernel(
    skip, where, cotangent, differ, h2, down, z, gz, dw_own, dw_other, db, sums, grad, h2t
):
    j = pl.program_id(0)
    blocks = lane_blocks(h2.shape[0])

    @pl.when(j == 0)
    def _():
        total = jnp.zeros((1, D), f32)
        for i in range(cotangent.shape[0] // TILE):
            rows = pl.ds(i * TILE, TILE)
            scale = per_row([kept(skip, i * GROUP + c, 1) for c in range(GROUP)], (TILE, 1))
            shift = per_row([differ[i, pl.ds(c, 1), :] for c in range(GROUP)], (TILE, D))
            value = (scale * (cotangent[rows, :].astype(f32) + (8.0 / S) * shift)).astype(bf16)
            grad[rows, :] = value
            total += jnp.sum(value.astype(f32), axis=0, keepdims=True)
        sums[...] = total
        square = (D, D)
        same = lax.broadcasted_iota(jnp.int32, square, 0) == lax.broadcasted_iota(jnp.int32, square, 1)
        eye = jnp.where(same, 1.0, 0.0).astype(bf16)
        for start, size in blocks:
            h2t[:, pl.ds(start, size)] = dot_nt(eye, h2[pl.ds(start, size), :]).astype(bf16)

    dw = db_sum = None
    for start, size in blocks:
        rows = pl.ds(start, size)
        hidden = z[rows, :].astype(f32)
        slope = (
            0.5 * (1.0 + lax.erf(hidden * 0.7071067811865476))
            + hidden * jnp.exp(-0.5 * hidden * hidden) * 0.3989422804014327
        )
        part = dot_nt(grad[rows, :], down[...]) * slope
        added = jnp.sum(part, axis=0, keepdims=True)
        db_sum = added if db_sum is None else db_sum + added
        part = part.astype(bf16)
        gz[rows, :] = part
        added = dot(h2t[:, rows], part)
        dw = added if dw is None else dw + added
    db[...] = db_sum
    unit = dw_own.shape[1]
    dw = dw.reshape(D // (2 * unit), 2, unit, dw.shape[1])
    dw_own[...] = jnp.where(where[0] == 0, dw[:, 0], dw[:, 1]).astype(bf16)
    dw_other[...] = jnp.where(where[0] == 0, dw[:, 1], dw[:, 0]).astype(bf16)


def hidden_backward(skip, core, cotangent, differ, h2, down, z, unit, after=()):
    rows = cotangent.shape[0]
    chunk = 512
    grads = (D // (2 * unit), unit)
    wide = pl.BlockSpec((rows, chunk), lambda j: (0, j))
    return call(
        hidden_backward_kernel,
        after,
        [
            smem(),
            smem(),
            resident((rows, D)),
            resident(differ.shape),
            resident((rows, D)),
            pl.BlockSpec((chunk, D), lambda j: (j, 0)),
            wide,
        ],
        (skip, jnp.reshape(core, (1,)).astype(jnp.int32), cotangent, differ, h2, down, z),
        vmem=60,
        grid=(DC // chunk,),
        out_specs=[
            wide,
            pl.BlockSpec(grads + (chunk,), lambda j: (0, 0, j)),
            pl.BlockSpec(grads + (chunk,), lambda j: (0, 0, j)),
            pl.BlockSpec((1, chunk), lambda j: (0, j)),
            pl.BlockSpec((1, D), lambda j: (0, 0)),
        ],
        out_shape=[
            jax.ShapeDtypeStruct((rows, DC), bf16),
            jax.ShapeDtypeStruct(grads + (DC,), bf16),
            jax.ShapeDtypeStruct(grads + (DC,), bf16),
            jax.ShapeDtypeStruct((1, DC), f32),
            jax.ShapeDtypeStruct((1, D), f32),
        ],
        scratch_shapes=[pltpu.VMEM((rows, D), bf16), pltpu.VMEM((D, rows), bf16)],
        cost_estimate=pl.CostEstimate(
            flops=4 * rows * D * DC, bytes_accessed=rows * DC * 4, transcendentals=0
        ),
        name="hidden_backward",
    )


def norm_back(grad, gain, normed, inv):
    scaled = grad * gain
    return inv * (
        scaled
        - jnp.mean(scaled, axis=-1, keepdims=True)
        - normed * jnp.mean(scaled * normed, axis=-1, keepdims=True)
    )


def last_backward_kernel(
    skip, gz, up, x1, cotangent, differ, x, act, slope, wd, wu, vecs, *rest, begin, first
):
    start, (out, dwd, dwu, sums, gh2, gx1, gv, h1, gh1) = rest[:-9], rest[-9:]
    i = pl.program_id(0)

    @pl.when(i == 0)
    def _():
        if first:
            dwd[...] = jnp.zeros_like(dwd)
            dwu[...] = jnp.zeros_like(dwu)
            sums[...] = jnp.zeros_like(sums)
        else:
            dwd[...] = start[1][...]
            dwu[...] = start[2][...]
            sums[...] = start[3][...]

    i += begin

    def add(row, value):
        sums[row : row + 1, :] += jnp.sum(value, axis=0, keepdims=True)

    block = TILE // 2
    for p in range(2):
        rows = pl.ds(p * block, block)
        gh2[rows, :] = dot_nt(gz[rows, :], up[...])
    for p in range(2):
        rows = pl.ds(p * block, block)
        grad = gh2[rows, :]
        normed, inv = normalize(x1[rows, :])
        add(2, grad * normed)
        add(3, grad)
        shift = per_row(
            [differ[0, pl.ds(c, 1), :] for c in range(GROUP)], (block, D), start=p * block
        )
        value = (
            cotangent[rows, :].astype(f32)
            + (8.0 / S) * shift
            + norm_back(grad, vecs[2:3, :], normed, inv)
        )
        gx1[rows, :] = value
        scale = per_row(
            [kept(skip, i * GROUP + c, 0) for c in range(GROUP)], (block, 1), start=p * block
        )
        gv[rows, :] = (scale * value).astype(bf16)

    normed, inv = normalize(x[...].astype(f32))
    h1[...] = (normed * vecs[0:1, :] + vecs[1:2, :]).astype(bf16)
    gh1[...] = jnp.zeros_like(gh1)
    ones = jnp.ones((ONES, D), bf16)
    for c in range(GROUP):
        rows = pl.ds(c * STEP, WIN)
        piece = gv[rows, :]
        dwd[c] += dot_nt(jnp.concatenate([act[c], ones], axis=0), piece)
        gu = (dot(wd[c], piece) * slope[c].astype(f32)).astype(bf16)
        dwu[c] += dot_nt(jnp.concatenate([h1[rows, :], ones], axis=0), gu)
        gh1[rows, :] += dot(wu[c], gu)
    grad = gh1[...]
    add(0, grad * normed)
    add(1, grad)
    out[...] = gx1[...] + norm_back(grad, vecs[0:1, :], normed, inv)


def last_backward(
    skip, gz, up, x1, cotangent, differ, x, act, slope, wd, wu, vecs, begin, count, before=None, after=()
):
    rows = x.shape[0]
    tile = pl.BlockSpec((TILE, D), lambda i: (i + begin, 0))
    hidden = pl.BlockSpec((GROUP, DS, D), lambda i: (i + begin, 0, 0))
    shapes = [(GROUP, DS + ONES, WIN), (GROUP, WIN + ONES, DS), (4, D)]
    extra = () if before is None else tuple(before)
    return call(
        functools.partial(last_backward_kernel, begin=begin, first=before is None),
        after,
        [
            smem(),
            pl.BlockSpec((TILE, DC), lambda i: (i + begin, 0)),
            resident((D, DC)),
            tile,
            tile,
            pl.BlockSpec((1, GROUP, D), lambda i: (i + begin, 0, 0)),
            tile,
            hidden,
            hidden,
            resident((GROUP, DS, WIN)),
            resident((GROUP, WIN, DS)),
            resident((4, D)),
        ]
        + ([] if before is None else [anywhere()] + [resident(s) for s in shapes]),
        (skip, gz, up, x1, cotangent, differ, x, act, slope, wd, wu, vecs) + extra,
        vmem=60,
        grid=(count,),
        out_specs=[
            tile,
            pl.BlockSpec(shapes[0], lambda i: (0, 0, 0)),
            pl.BlockSpec(shapes[1], lambda i: (0, 0, 0)),
            pl.BlockSpec(shapes[2], lambda i: (0, 0)),
        ],
        out_shape=[jax.ShapeDtypeStruct((rows, D), f32)] + [jax.ShapeDtypeStruct(s, f32) for s in shapes],
        scratch_shapes=[
            pltpu.VMEM((TILE, D), f32),
            pltpu.VMEM((TILE, D), f32),
            pltpu.VMEM((TILE, D), bf16),
            pltpu.VMEM((TILE, D), bf16),
            pltpu.VMEM((TILE, D), f32),
        ],
        input_output_aliases={} if before is None else {12: 0},
        cost_estimate=pl.CostEstimate(
            flops=count * TILE * (2 * D * DC + 20 * DS * D),
            bytes_accessed=count * TILE * (DC * 2 + D * 24),
            transcendentals=0,
        ),
        name="last_backward",
    )


def merge_kernel(where, low, high, low_in, high_in, sums, shift, out):
    i = pl.program_id(0)
    half = pl.num_programs(0) // 2
    for k in range(low.shape[0]):
        added = dot(sums[k], shift[...])
        own = jnp.where(i < half, low[k, 0], high[k, 0]).astype(f32)
        got = jnp.where(i < half, low_in[k], high_in[k]).astype(f32)
        out[k] = (own + got + added).astype(bf16)


def merge(core, low, high, low_in, high_in, sums, shift):
    half, _, rows, _ = low.shape
    block = min(4, half)
    steps = half // block
    first = lambda i: jnp.minimum(i, steps - 1)
    second = lambda i: jnp.maximum(i - steps, 0)
    return pl.pallas_call(
        merge_kernel,
        grid_spec=pltpu.PrefetchScalarGridSpec(
            num_scalar_prefetch=1,
            grid=(2 * steps,),
            in_specs=[
                pl.BlockSpec((block, 1, rows, D), lambda i, w: (first(i), w[0], 0, 0)),
                pl.BlockSpec((block, 1, rows, D), lambda i, w: (second(i), w[0], 0, 0)),
                pl.BlockSpec((block, rows, D), lambda i, w: (first(i), 0, 0)),
                pl.BlockSpec((block, rows, D), lambda i, w: (second(i), 0, 0)),
                pl.BlockSpec((block,) + sums.shape[1:], lambda i, w: (i, 0, 0)),
                pl.BlockSpec(shift.shape, lambda i, w: (0, 0)),
            ],
            out_specs=pl.BlockSpec((block, rows, D), lambda i, w: (i, 0, 0)),
        ),
        out_shape=jax.ShapeDtypeStruct((2 * half, rows, D), bf16),
        compiler_params=pltpu.CompilerParams(vmem_limit_bytes=24 * MIB),
        name="merge",
    )(jnp.reshape(core, (1,)).astype(jnp.int32), low, high, low_in, high_in, sums, shift)


def place_kernel(where, *refs, shape):
    pieces, (kz, ky, kx) = shape
    out = refs[-1]
    for k, (places, column) in enumerate(pieces):
        own, other = refs[2 * k], refs[2 * k + 1]
        rows, cols = own.shape[-2:]
        for index, (z, y, x) in places:
            chip = ((where[0] ^ z) * ky + (where[1] ^ y)) * kx + (where[2] ^ x)
            if rows % 16 == 0:
                for ref, core in ((own, where[3]), (other, 1 - where[3])):
                    start = pl.multiple_of((chip * 2 + core) * rows, rows)
                    out[pl.ds(start, rows), pl.ds(column, cols)] = ref[index]
            else:
                both = [own[index].astype(f32), other[index].astype(f32)]
                low = jnp.where(where[3] == 0, both[0], both[1])
                high = jnp.where(where[3] == 0, both[1], both[0])
                start = pl.multiple_of(chip * 2 * rows, 2 * rows)
                value = jnp.concatenate([low, high], axis=0).astype(bf16)
                out[pl.ds(start, 2 * rows), pl.ds(column, cols)] = value


def behind(value, *others):
    return lax.optimization_barrier((value,) + others)[0]


class Net:
    def __init__(self, n):
        chips = n // 2
        side = 1
        while 2 * side * side * side < chips:
            side *= 2
        if 2 * side * side * side != chips:
            raise ValueError("unknown slice")
        self.n, self.side, self.chips = n, side, chips
        self.core = [1]
        self.xy = [2 * k for k in range(1, side * side)]
        self.x = [2 * k for k in range(1, side)]
        self.y = [2 * side * k for k in range(1, side)]
        self.z = [2 * side * side * k for k in range(1, 2 * side)]
        self.me = lax.axis_index("dp")
        self.at_core = self.me % 2
        self.at_xy = (self.me // 2) % (side * side)
        self.at_x = (self.me // 2) % side
        self.at_y = (self.me // (2 * side)) % side
        self.at_z = self.me // (2 * side * side)

    def swap(self, value, offset):
        return lax.ppermute(value, "dp", [(i, i ^ offset) for i in range(self.n)])

    def spread(self, value, offsets):
        return jnp.stack([value] + [self.swap(value, o) for o in offsets])

    def gather_small(self, value, beside=()):
        held = value
        order = np.zeros((1,), np.int64)
        steps = []
        for k, offsets in enumerate((self.z, self.xy, self.core)):
            held = self.spread(held, offsets)
            if k < len(beside):
                held = behind(held, beside[k])
            steps.append(held)
            order = (np.array([0] + offsets)[:, None] + order[None, :]).reshape(-1)
        return held.reshape((self.n,) + value.shape), order, steps

    def plane(self, stacked):
        side = self.side
        places = [(z, 0, 0) for z in range(2 * side)]
        out = [(stacked, places, 0)]
        for k, offset in enumerate(self.xy):
            y, x = divmod(k + 1, side)
            out.append((self.swap(stacked, offset), [(z, y, x) for z, _, _ in places], 0))
        return out

    def plane_by_halves(self, stacked):
        side, kz = self.side, 2 * self.side
        cols = stacked.shape[-1] // 2
        out = []
        for half, (one, two) in enumerate(((self.y, self.x), (self.x, self.y))):
            held = self.spread(stacked[:, :, half * cols : (half + 1) * cols], one)
            for k in range(side):
                place = lambda a, b: (a, b) if half == 0 else (b, a)
                places = [(z,) + place(j, k) for j in range(side) for z in range(kz)]
                got = held if k == 0 else self.swap(held, two[k - 1])
                out.append((got.reshape((side * kz,) + got.shape[2:]), places, half * cols))
        return out

    def place(self, parts, after=()):
        side, kz = self.side, 2 * self.side
        rows = parts[0][0].shape[1]
        width = max(column + blocks.shape[2] for blocks, _, column in parts)
        parts = [(behind(blocks, *after), places, column) for blocks, places, column in parts]
        pairs = [(blocks, self.swap(blocks, 1)) for blocks, _, _ in parts]
        shape = (self.n * rows, width)
        if rows % 8 == 0:
            spec = tuple((list(enumerate(places)), column) for _, places, column in parts)
            where = jnp.stack([self.at_z, self.at_y, self.at_x, self.at_core]).astype(jnp.int32)
            inputs = [v for pair in pairs for v in pair]
            return call(
                lambda *refs: place_kernel(*refs, shape=(spec, (kz, side, side))),
                after,
                [smem()] + [pl.BlockSpec(memory_space=pltpu.VMEM)] * len(inputs),
                (where, *inputs),
                vmem=20,
                out_specs=pl.BlockSpec(memory_space=pltpu.VMEM),
                out_shape=jax.ShapeDtypeStruct(shape, bf16),
                name="place",
            )
        columns = {}
        for (blocks, places, column), pair in zip(parts, pairs):
            columns.setdefault(column, []).extend(
                (core, place, pair[core][k]) for k, place in enumerate(places) for core in (0, 1)
            )
        out = []
        for column in sorted(columns):
            blocks = sorted(columns[column], key=lambda b: (b[1], b[0]))
            held = jnp.stack([b[2] for b in blocks]).reshape(kz, side, side, 2, rows, -1)
            for axis, at in enumerate((self.at_z, self.at_y, self.at_x, self.at_core)):
                held = jnp.take(held, jnp.arange(held.shape[axis]) ^ at, axis=axis)
            out.append(held.reshape(shape[0], -1))
        return jnp.concatenate(out, axis=1)

    def pick(self, value, index, axis):
        return lax.dynamic_index_in_dim(value, index, axis, keepdims=False)

    def start_axis(self, value, axis, at, offsets):
        own = self.pick(value, at, axis)
        return [own] + [
            self.swap(self.pick(value, at ^ (k + 1), axis).astype(bf16), o) for k, o in enumerate(offsets)
        ]

    def finish_axis(self, parts):
        parts = [p.astype(f32) for p in parts]
        while len(parts) > 1:
            parts = [parts[k] + parts[k + 1] for k in range(0, len(parts), 2)]
        return parts[0]

    def scatter_small(self, value):
        kz, k = 2 * self.side, self.side
        value = value.reshape(kz, k * k, 2, -1)
        value = self.finish_axis(self.start_axis(value, 2, self.at_core, self.core)).astype(bf16)
        value = self.finish_axis(self.start_axis(value, 1, self.at_xy, self.xy)).astype(bf16)
        return self.finish_axis(self.start_axis(value, 0, self.at_z, self.z))


def shifted(matrix, axis):
    out = []
    for c in range(GROUP):
        pads = [(0, 0)] * matrix.ndim
        pads[axis] = (4 * c, WIN - S - 4 * c)
        out.append(jnp.pad(matrix, pads))
    return jnp.stack(out)


def per_device(
    tokens,
    cotangent,
    skip_mask,
    pair_index,
    patch_up,
    patch_down,
    channel_up,
    channel_down,
    patch_upbias,
    patch_downbias,
    first_gain,
    first_shift,
    second_gain,
    second_shift,
    channel_upbias,
    channel_downbias,
    devices,
):
    net = Net(devices)
    chips = devices // 2
    core = net.at_core
    rows = tokens.shape[0]
    crops = rows // S
    unit_d = D // devices
    unit_h = DC // devices
    kz, kxy = 2 * net.side, net.side * net.side

    small = [
        patch_up, patch_down, first_gain, first_shift, second_gain, second_shift, channel_upbias, channel_downbias,
    ]
    sizes = [v.shape[0] for v in small]
    length = sum(sizes)
    padded = -(-length // 1024) * 1024
    packed = join(small, 0, padded)
    every, order, _ = net.gather_small(packed)
    in_order = (jnp.arange(devices)[:, None] ^ net.me) == jnp.asarray(order, jnp.int32)[None, :]
    every = dot(in_order.astype(bf16), every).astype(bf16)
    ends = np.cumsum([0] + sizes)
    up_token = every[:, : ends[1]].reshape(S, DS)
    down_token = every[:, ends[1] : ends[2]].reshape(DS, S)
    vecs = every[:, ends[2] : ends[6]].astype(f32).reshape(devices, 4, unit_d).transpose(1, 0, 2).reshape(4, D)
    bias_hidden = every[:, ends[6] : ends[7]].astype(f32).reshape(1, DC)
    bias_out = every[:, ends[7] : ends[8]].astype(f32).reshape(1, D)

    up_stack = net.spread(channel_up.reshape(unit_d, DC), net.z)
    down_stack = net.spread(behind(channel_down.reshape(unit_h, D), up_stack), net.z)
    up_parts = net.plane_by_halves(up_stack)
    down_stack = behind(down_stack, up_parts[0][0], up_parts[net.side][0])
    down_parts = net.plane(down_stack)

    up_pad = shifted(up_token, 0)
    down_pad = shifted(down_token, 1)
    x1, h2, act_t, slope_t = token_forward(
        skip_mask,
        tokens,
        up_pad.transpose(0, 2, 1),
        down_pad.transpose(0, 2, 1),
        patch_upbias.astype(f32).reshape(DS, 1),
        shifted(patch_downbias.astype(f32).reshape(S, 1), 0),
        vecs,
        after=(down_stack,),
    )
    up = net.place(up_parts, after=(h2,))
    down = net.place(down_parts, after=(h2,))
    other_pairs, other_skip = net.swap(pair_index, 1), net.swap(skip_mask[:, 1], 1)
    outputs, scaled, act_low, act_high, z, act_sums, pooled = channel_forward(
        skip_mask, h2, up, down, x1, bias_hidden, bias_out, cotangent, after=(other_pairs, other_skip)
    )
    pooled = pooled.reshape(crops, D)

    chip_sums = net.start_axis(act_sums.reshape(crops, chips, 2, unit_h), 2, core, net.core)
    chip_sums = jnp.concatenate([v.astype(bf16).reshape(crops, -1) for v in chip_sums])
    chip_sums = chip_sums.reshape(2 * crops, chips, unit_h).transpose(1, 2, 0)

    def grad_down(act):
        value = lax.dot_general(act, scaled, (((0,), (0,)), ((), ())), preferred_element_type=f32)
        return value.astype(bf16).reshape(chips // 2, 2, unit_h, D)

    low, high = grad_down(act_low), grad_down(act_high)
    every, order, steps = net.gather_small(pooled.astype(bf16), beside=(low, high))
    every = every.reshape(-1, D)
    low, high = behind(low, steps[1]), behind(high, steps[1])
    received = [net.swap(net.pick(v, 1 - core, 1), 1) for v in (low, high)]
    codes = (order[:, None] * crops + np.arange(crops)[None, :]).reshape(1, -1)
    flip = net.me.astype(jnp.int32) * crops
    find = lambda index: ((index.reshape(-1, 1) ^ flip) == jnp.asarray(codes, jnp.int32)).astype(bf16)
    partner = dot(find(jnp.stack([pair_index, other_pairs])), every)
    differ = pooled - partner[:crops]
    own_code = jnp.stack([net.me, net.me ^ 1]).astype(jnp.int32)[:, None] * crops + jnp.arange(crops, dtype=jnp.int32)
    chip_differ = dot(find(own_code), every) - partner
    losses = 2.0 * jnp.sum(differ * differ, axis=1)
    differ = differ.reshape(crops // GROUP, GROUP, D)

    chip_keep = jnp.stack([skip_mask[:, 1], other_skip]).astype(f32).reshape(-1, 1) * keep_scale
    chip_shift = (chip_keep * (8.0 / S) * chip_differ).astype(bf16)
    down_sum = merge(core, low, high, *received, chip_sums, chip_shift)
    down_parts = net.start_axis(down_sum.reshape(kz, kxy, unit_h, D), 1, net.at_xy, net.xy)

    gz, up_own, up_other, grad_bias_hidden, grad_bias_out = hidden_backward(
        skip_mask, core, cotangent, differ, h2, down, z, unit_d, after=(down_sum,)
    )
    down_sum = net.finish_axis(down_parts)
    up_other = net.swap(behind(up_other, down_sum), 1)
    down_parts = net.start_axis(down_sum, 0, net.at_z, net.z)
    tiles = rows // TILE
    cuts = (0, 1, tiles - 1, tiles)
    passed = (
        skip_mask, gz, up, x1, cotangent, differ, tokens, act_t, slope_t, down_pad, up_pad, vecs
    )
    done = last_backward(*passed, cuts[0], cuts[1] - cuts[0], after=(down_sum,))
    up_sum = (up_own.astype(f32) + behind(up_other, done[3]).astype(f32)).astype(bf16)
    down_grad = net.finish_axis([behind(v, done[3]) for v in down_parts]).reshape(-1)
    up_parts = net.start_axis(up_sum.reshape(kz, kxy, unit_d, DC), 1, net.at_xy, net.xy)
    done = last_backward(*passed, cuts[1], cuts[2] - cuts[1], before=done, after=(up_sum, down_grad))
    up_sum = net.finish_axis([behind(v, done[3]) for v in up_parts])
    up_parts = net.start_axis(up_sum, 0, net.at_z, net.z)
    grad_tokens, dwd, dwu, sums = last_backward(
        *passed, cuts[2], cuts[3] - cuts[2], before=done, after=(up_sum,)
    )
    up_parts, dwd, dwu, sums = lax.optimization_barrier((up_parts, dwd, dwu, sums))
    up_grad = net.finish_axis(up_parts).reshape(-1)

    grad_patch_up = sum(dwu[c, 4 * c : 4 * c + S] for c in range(GROUP))
    grad_patch_down = sum(dwd[c, :DS, 4 * c : 4 * c + S] for c in range(GROUP))
    bias_up = sum(dwu[c, WIN] for c in range(GROUP))
    bias_down = sum(dwd[c, DS, 4 * c : 4 * c + S] for c in range(GROUP))
    scattered = [
        grad_patch_up, grad_patch_down, sums[0], sums[1], sums[2], sums[3], grad_bias_hidden, grad_bias_out
    ]
    scattered = [v.reshape(devices, -1) for v in scattered]
    scattered += [jnp.broadcast_to(v, (devices,) + v.shape) for v in (bias_up, bias_down)]
    total = sum(v.shape[1] for v in scattered)
    scattered = join([v.astype(bf16) for v in scattered], 1, -(-total // 1024) * 1024)
    own = net.scatter_small(scattered)
    ends = np.cumsum([0] + sizes + [DS, S])
    grads = [own[a:b] for a, b in zip(ends[:-1], ends[1:])]
    return (
        outputs, losses, grad_tokens, grads[0], grads[1], up_grad, down_grad, grads[8], grads[9], *grads[2:8],
    )


def solution(mesh):
    row, flat, whole = P("dp", None), P("dp"), P()
    return jax.shard_map(
        functools.partial(per_device, devices=mesh.shape["dp"]),
        mesh=mesh,
        in_specs=(row, row, row, flat, flat, flat, flat, flat, whole, whole) + (flat,) * 6,
        out_specs=(row, flat, row, flat, flat, flat, flat, whole, whole) + (flat,) * 6,
        check_vma=False,
    )
```

```python
import functools

import jax
import jax.numpy as jnp
import numpy as np
from jax import lax
from jax.experimental import pallas as pl
from jax.experimental.pallas import tpu as pltpu
from jax.sharding import PartitionSpec as P

D = 768
S = 196
DS = 384
DC = 3072

GROUP = 4
TILE = GROUP * S
WIN = 208
STEP = 192
ONES = 16

eps_norm = 1e-06
keep_scale = 4.0 / 3.0
f32 = jnp.float32
bf16 = jnp.bfloat16
MIB = 1024 * 1024


def resident(shape):
    zeros = (0,) * len(shape)
    return pl.BlockSpec(shape, lambda *_: zeros, pipeline_mode=pl.Buffered(1))


def smem():
    return pl.BlockSpec(memory_space=pltpu.SMEM)


def anywhere():
    return pl.BlockSpec(memory_space=pl.ANY)


def call(kernel, after, in_specs, args, vmem, **rest):
    count = len(args)

    def body(*refs):
        kernel(*refs[:count], *refs[count + len(after) :])

    return pl.pallas_call(
        body,
        in_specs=list(in_specs) + [anywhere()] * len(after),
        compiler_params=pltpu.CompilerParams(vmem_limit_bytes=vmem * MIB),
        **rest,
    )(*args, *after)


def kept(skip, crop, branch):
    return skip[crop, branch].astype(f32) * keep_scale


def dot(a, b):
    return jnp.dot(a, b, preferred_element_type=f32)


def dot_nt(a, b):
    return lax.dot_general(a, b, (((1,), (1,)), ((), ())), preferred_element_type=f32)


def gelu_and_slope(z):
    phi = 0.5 * (1.0 + lax.erf(z * 0.7071067811865476))
    return z * phi, phi + z * jnp.exp(-0.5 * z * z) * 0.3989422804014327


def normalize(v):
    center = v - jnp.mean(v, axis=-1, keepdims=True)
    inv = lax.rsqrt(jnp.mean(center * center, axis=-1, keepdims=True) + eps_norm)
    return center * inv, inv


def join(values, axis, total):
    out, start = None, 0
    for v in values:
        pads = [(0, 0)] * v.ndim
        pads[axis] = (start, total - start - v.shape[axis])
        start += v.shape[axis]
        v = jnp.pad(v, pads)
        out = v if out is None else out + v
    return out


def per_row(values, shape, start=0):
    rows = lax.broadcasted_iota(jnp.int32, shape, 0) + start
    out = jnp.broadcast_to(values[GROUP - 1], shape)
    for c in range(GROUP - 2, -1, -1):
        out = jnp.where(rows < (c + 1) * S, values[c], out)
    return out


def crop_sum(read, c):
    lo, hi = c * S, (c + 1) * S
    base = c * STEP
    width = read(base, 8).shape[1]
    total = jnp.sum(read(base + 16, STEP - 16), axis=0, keepdims=True)
    for piece in (base, base + STEP):
        rows = lax.broadcasted_iota(jnp.int32, (16, width), 0) + piece
        ok = (rows >= lo) & (rows < hi)
        total += jnp.sum(jnp.where(ok, read(piece, 16), 0.0), axis=0, keepdims=True)
    return total


def window_matrix(c, shape):
    return jnp.where(
        lax.broadcasted_iota(jnp.int32, shape, 0) == lax.broadcasted_iota(jnp.int32, shape, 1) + 4 * c, 1.0, 0.0
    ).astype(bf16)


def token_forward_kernel(skip, x, wu, wd, bu, bd, vecs, x1_out, h2, act, slope, wu_out, wd_out, h1, x1, wut, wdt, bdt):
    i = pl.program_id(0)

    @pl.when(i == 0)
    def _():
        for c in range(GROUP):
            move = window_matrix(c, (WIN, S))
            wu_out[c] = dot(move, wu[...]).astype(bf16)
            wut[c] = lax.dot_general(
                wu[...], move, (((0,), (1,)), ((), ())), preferred_element_type=f32
            ).astype(bf16)
            wd_out[c] = dot_nt(wd[...], move).astype(bf16)
            wdt[c] = dot_nt(move, wd[...]).astype(bf16)
            bdt[c] = jnp.sum(move.astype(f32) * bd[...], axis=1, keepdims=True)

    tokens = x[...].astype(f32)
    normed, _ = normalize(tokens)
    h1[...] = (normed * vecs[0:1, :] + vecs[1:2, :]).astype(bf16)
    x1[...] = tokens
    for c in range(GROUP):
        lifted = dot(wut[c], h1[pl.ds(c * STEP, WIN), :]) + bu[...]
        value, grad = gelu_and_slope(lifted)
        value = value.astype(bf16)
        act[c] = value
        slope[c] = grad.astype(bf16)
        mixed = dot(wdt[c], value) + bdt[c]
        x1[pl.ds(c * STEP, WIN), :] += kept(skip, i * GROUP + c, 0) * mixed
    x1_out[...] = x1[...].astype(bf16)
    normed, _ = normalize(x1[...])
    h2[...] = (normed * vecs[2:3, :] + vecs[3:4, :]).astype(bf16)


def token_forward(skip, x, wu, wd, bu, bd, vecs, after=()):
    rows = x.shape[0]
    crops = rows // S
    tile = pl.BlockSpec((TILE, D), lambda i: (i, 0))
    hidden = pl.BlockSpec((GROUP, DS, D), lambda i: (i, 0, 0))
    moved = [(GROUP, WIN, DS), (GROUP, DS, WIN)]
    return call(
        token_forward_kernel,
        after,
        [
            smem(),
            tile,
            resident((S, DS)),
            resident((DS, S)),
            resident((DS, 1)),
            resident((1, S)),
            resident((4, D)),
        ],
        (skip, x, wu, wd, bu, bd, vecs),
        vmem=50,
        grid=(rows // TILE,),
        out_specs=[tile, tile, hidden, hidden] + [pl.BlockSpec(m, lambda i: (0, 0, 0)) for m in moved],
        out_shape=[
            jax.ShapeDtypeStruct((rows, D), bf16),
            jax.ShapeDtypeStruct((rows, D), bf16),
            jax.ShapeDtypeStruct((crops, DS, D), bf16),
            jax.ShapeDtypeStruct((crops, DS, D), bf16),
        ]
        + [jax.ShapeDtypeStruct(m, bf16) for m in moved],
        scratch_shapes=[
            pltpu.VMEM((TILE, D), bf16),
            pltpu.VMEM((TILE, D), f32),
            pltpu.VMEM((GROUP, DS, WIN), bf16),
            pltpu.VMEM((GROUP, WIN, DS), bf16),
            pltpu.VMEM((GROUP, WIN, 1), f32),
        ],
        cost_estimate=pl.CostEstimate(
            flops=20 * rows * DS * D, bytes_accessed=rows * D * 12, transcendentals=0
        ),
        name="token_forward",
    )


def hidden_kernel(h2, up, bias, act_low, act_high, z_out, sums):
    chunk = 512
    count = DC // chunk
    for j in range(count):
        cols = pl.ds(j * chunk, chunk)
        z = dot(h2[...], up[:, cols]) + bias[:, cols]
        z_out[:, cols] = z.astype(bf16)
        value = z * (0.5 * (1.0 + lax.erf(z * 0.7071067811865476)))
        half, k = divmod(j, count // 2)
        (act_low, act_high)[half][:, pl.ds(k * chunk, chunk)] = value.astype(bf16)
        for c in range(GROUP):
            sums[0, pl.ds(c, 1), cols] = crop_sum(lambda a, n: value[a : a + n], c)


def hidden_forward(h2, up, bias, after=()):
    rows = h2.shape[0]
    grid = rows // TILE
    half = pl.BlockSpec((TILE, DC // 2), lambda i: (i, 0))
    return call(
        hidden_kernel,
        after,
        [pl.BlockSpec((TILE, D), lambda i: (i, 0)), resident((D, DC)), resident((1, DC))],
        (h2, up, bias),
        vmem=60,
        grid=(grid,),
        out_specs=[
            half,
            half,
            pl.BlockSpec((TILE, DC), lambda i: (i, 0)),
            pl.BlockSpec((1, GROUP, DC), lambda i: (i, 0, 0)),
        ],
        out_shape=[
            jax.ShapeDtypeStruct((rows, DC // 2), bf16),
            jax.ShapeDtypeStruct((rows, DC // 2), bf16),
            jax.ShapeDtypeStruct((rows, DC), bf16),
            jax.ShapeDtypeStruct((grid, GROUP, DC), f32),
        ],
        cost_estimate=pl.CostEstimate(
            flops=3 * rows * D * DC, bytes_accessed=rows * DC * 4, transcendentals=0
        ),
        name="hidden_forward",
    )


def output_kernel(skip, act_low, act_high, down, x1, bias, cotangent, out, scaled, pooled):
    i = pl.program_id(0)
    scale = per_row([kept(skip, i * GROUP + c, 1) for c in range(GROUP)], (TILE, 1))
    branch = dot(act_low[...], down[pl.ds(0, DC // 2), :]) + bias[...]
    branch += dot(act_high[...], down[pl.ds(DC // 2, DC // 2), :])
    y = x1[...].astype(f32) + scale * branch
    out[...] = y.astype(bf16)
    scaled[...] = (scale * cotangent[...].astype(f32)).astype(bf16)
    for c in range(GROUP):
        pooled[0, pl.ds(c, 1), :] = crop_sum(lambda a, n: y[a : a + n], c) * (1.0 / S)


def output_forward(skip, act_low, act_high, down, x1, bias, cotangent, after=()):
    rows = x1.shape[0]
    grid = rows // TILE
    tile = pl.BlockSpec((TILE, D), lambda i: (i, 0))
    half = pl.BlockSpec((TILE, DC // 2), lambda i: (i, 0))
    return call(
        output_kernel,
        after,
        [smem(), half, half, resident((DC, D)), tile, resident((1, D)), tile],
        (skip, act_low, act_high, down, x1, bias, cotangent),
        vmem=60,
        grid=(grid,),
        out_specs=[tile, tile, pl.BlockSpec((1, GROUP, D), lambda i: (i, 0, 0))],
        out_shape=[
            jax.ShapeDtypeStruct((rows, D), bf16),
            jax.ShapeDtypeStruct((rows, D), bf16),
            jax.ShapeDtypeStruct((grid, GROUP, D), f32),
        ],
        cost_estimate=pl.CostEstimate(
            flops=2 * rows * D * DC, bytes_accessed=rows * DC * 2 + rows * D * 10, transcendentals=0
        ),
        name="output_forward",
    )


def lane_blocks(rows):
    count = max(rows // 768, 1)
    return [(k * 768, 768 if k < count - 1 else rows - 768 * (count - 1)) for k in range(count)]


def hidden_backward_kernel(
    skip, where, cotangent, differ, h2, down, z, gz, dw_own, dw_other, db, sums, grad, h2t
):
    j = pl.program_id(0)
    blocks = lane_blocks(h2.shape[0])

    @pl.when(j == 0)
    def _():
        total = jnp.zeros((1, D), f32)
        for i in range(cotangent.shape[0] // TILE):
            rows = pl.ds(i * TILE, TILE)
            scale = per_row([kept(skip, i * GROUP + c, 1) for c in range(GROUP)], (TILE, 1))
            shift = per_row([differ[i, pl.ds(c, 1), :] for c in range(GROUP)], (TILE, D))
            value = (scale * (cotangent[rows, :].astype(f32) + (8.0 / S) * shift)).astype(bf16)
            grad[rows, :] = value
            total += jnp.sum(value.astype(f32), axis=0, keepdims=True)
        sums[...] = total
        square = (D, D)
        same = lax.broadcasted_iota(jnp.int32, square, 0) == lax.broadcasted_iota(jnp.int32, square, 1)
        eye = jnp.where(same, 1.0, 0.0).astype(bf16)
        for start, size in blocks:
            h2t[:, pl.ds(start, size)] = dot_nt(eye, h2[pl.ds(start, size), :]).astype(bf16)

    dw = db_sum = None
    for start, size in blocks:
        rows = pl.ds(start, size)
        hidden = z[rows, :].astype(f32)
        slope = (
            0.5 * (1.0 + lax.erf(hidden * 0.7071067811865476))
            + hidden * jnp.exp(-0.5 * hidden * hidden) * 0.3989422804014327
        )
        part = dot_nt(grad[rows, :], down[...]) * slope
        added = jnp.sum(part, axis=0, keepdims=True)
        db_sum = added if db_sum is None else db_sum + added
        part = part.astype(bf16)
        gz[rows, :] = part
        added = dot(h2t[:, rows], part)
        dw = added if dw is None else dw + added
    db[...] = db_sum
    unit = dw_own.shape[1]
    dw = dw.reshape(D // (2 * unit), 2, unit, dw.shape[1])
    dw_own[...] = jnp.where(where[0] == 0, dw[:, 0], dw[:, 1]).astype(bf16)
    dw_other[...] = jnp.where(where[0] == 0, dw[:, 1], dw[:, 0]).astype(bf16)


def hidden_backward(skip, core, cotangent, differ, h2, down, z, unit, after=()):
    rows = cotangent.shape[0]
    chunk = 512
    grads = (D // (2 * unit), unit)
    wide = pl.BlockSpec((rows, chunk), lambda j: (0, j))
    return call(
        hidden_backward_kernel,
        after,
        [
            smem(),
            smem(),
            resident((rows, D)),
            resident(differ.shape),
            resident((rows, D)),
            pl.BlockSpec((chunk, D), lambda j: (j, 0)),
            wide,
        ],
        (skip, jnp.reshape(core, (1,)).astype(jnp.int32), cotangent, differ, h2, down, z),
        vmem=52,
        grid=(DC // chunk,),
        out_specs=[
            wide,
            pl.BlockSpec(grads + (chunk,), lambda j: (0, 0, j)),
            pl.BlockSpec(grads + (chunk,), lambda j: (0, 0, j)),
            pl.BlockSpec((1, chunk), lambda j: (0, j)),
            pl.BlockSpec((1, D), lambda j: (0, 0)),
        ],
        out_shape=[
            jax.ShapeDtypeStruct((rows, DC), bf16),
            jax.ShapeDtypeStruct(grads + (DC,), bf16),
            jax.ShapeDtypeStruct(grads + (DC,), bf16),
            jax.ShapeDtypeStruct((1, DC), f32),
            jax.ShapeDtypeStruct((1, D), f32),
        ],
        scratch_shapes=[pltpu.VMEM((rows, D), bf16), pltpu.VMEM((D, rows), bf16)],
        cost_estimate=pl.CostEstimate(
            flops=4 * rows * D * DC, bytes_accessed=rows * DC * 4, transcendentals=0
        ),
        name="hidden_backward",
    )


def norm_back(grad, gain, normed, inv):
    scaled = grad * gain
    return inv * (
        scaled
        - jnp.mean(scaled, axis=-1, keepdims=True)
        - normed * jnp.mean(scaled * normed, axis=-1, keepdims=True)
    )


def last_backward_kernel(
    skip, gz, up, x1, cotangent, differ, x, act, slope, wd, wu, vecs, *rest, begin, first
):
    start, (out, dwd, dwu, sums, gh2, gx1, gv, h1, gh1) = rest[:-9], rest[-9:]
    i = pl.program_id(0)

    @pl.when(i == 0)
    def _():
        if first:
            dwd[...] = jnp.zeros_like(dwd)
            dwu[...] = jnp.zeros_like(dwu)
            sums[...] = jnp.zeros_like(sums)
        else:
            dwd[...] = start[1][...]
            dwu[...] = start[2][...]
            sums[...] = start[3][...]

    i += begin

    def add(row, value):
        sums[row : row + 1, :] += jnp.sum(value, axis=0, keepdims=True)

    block = TILE // 2
    for p in range(2):
        rows = pl.ds(p * block, block)
        gh2[rows, :] = dot_nt(gz[rows, :], up[...])
    for p in range(2):
        rows = pl.ds(p * block, block)
        grad = gh2[rows, :]
        normed, inv = normalize(x1[rows, :].astype(f32))
        add(2, grad * normed)
        add(3, grad)
        shift = per_row(
            [differ[0, pl.ds(c, 1), :] for c in range(GROUP)], (block, D), start=p * block
        )
        value = (
            cotangent[rows, :].astype(f32)
            + (8.0 / S) * shift
            + norm_back(grad, vecs[2:3, :], normed, inv)
        )
        gx1[rows, :] = value
        scale = per_row(
            [kept(skip, i * GROUP + c, 0) for c in range(GROUP)], (block, 1), start=p * block
        )
        gv[rows, :] = (scale * value).astype(bf16)

    normed, inv = normalize(x[...].astype(f32))
    h1[...] = (normed * vecs[0:1, :] + vecs[1:2, :]).astype(bf16)
    gh1[...] = jnp.zeros_like(gh1)
    ones = jnp.ones((ONES, D), bf16)
    for c in range(GROUP):
        rows = pl.ds(c * STEP, WIN)
        piece = gv[rows, :]
        dwd[c] += dot_nt(jnp.concatenate([act[c], ones], axis=0), piece)
        gu = (dot(wd[c], piece) * slope[c].astype(f32)).astype(bf16)
        dwu[c] += dot_nt(jnp.concatenate([h1[rows, :], ones], axis=0), gu)
        gh1[rows, :] += dot(wu[c], gu)
    grad = gh1[...]
    add(0, grad * normed)
    add(1, grad)
    out[...] = gx1[...] + norm_back(grad, vecs[0:1, :], normed, inv)


def last_backward(
    skip, gz, up, x1, cotangent, differ, x, act, slope, wd, wu, vecs, begin, count, before=None, after=()
):
    rows = x.shape[0]
    tile = pl.BlockSpec((TILE, D), lambda i: (i + begin, 0))
    hidden = pl.BlockSpec((GROUP, DS, D), lambda i: (i + begin, 0, 0))
    shapes = [(GROUP, DS + ONES, WIN), (GROUP, WIN + ONES, DS), (4, D)]
    extra = () if before is None else tuple(before)
    return call(
        functools.partial(last_backward_kernel, begin=begin, first=before is None),
        after,
        [
            smem(),
            pl.BlockSpec((TILE, DC), lambda i: (i + begin, 0)),
            resident((D, DC)),
            tile,
            tile,
            pl.BlockSpec((1, GROUP, D), lambda i: (i + begin, 0, 0)),
            tile,
            hidden,
            hidden,
            resident((GROUP, DS, WIN)),
            resident((GROUP, WIN, DS)),
            resident((4, D)),
        ]
        + ([] if before is None else [anywhere()] + [resident(s) for s in shapes]),
        (skip, gz, up, x1, cotangent, differ, x, act, slope, wd, wu, vecs) + extra,
        vmem=48,
        grid=(count,),
        out_specs=[
            tile,
            pl.BlockSpec(shapes[0], lambda i: (0, 0, 0)),
            pl.BlockSpec(shapes[1], lambda i: (0, 0, 0)),
            pl.BlockSpec(shapes[2], lambda i: (0, 0)),
        ],
        out_shape=[jax.ShapeDtypeStruct((rows, D), f32)] + [jax.ShapeDtypeStruct(s, f32) for s in shapes],
        scratch_shapes=[
            pltpu.VMEM((TILE, D), f32),
            pltpu.VMEM((TILE, D), f32),
            pltpu.VMEM((TILE, D), bf16),
            pltpu.VMEM((TILE, D), bf16),
            pltpu.VMEM((TILE, D), f32),
        ],
        input_output_aliases={} if before is None else {12: 0},
        cost_estimate=pl.CostEstimate(
            flops=count * TILE * (2 * D * DC + 20 * DS * D),
            bytes_accessed=count * TILE * (DC * 2 + D * 24),
            transcendentals=0,
        ),
        name="last_backward",
    )


def merge_kernel(where, low, high, low_in, high_in, sums, shift, out):
    i = pl.program_id(0)
    half = pl.num_programs(0) // 2
    for k in range(low.shape[0]):
        added = dot(sums[k], shift[...])
        own = jnp.where(i < half, low[k, 0], high[k, 0]).astype(f32)
        got = jnp.where(i < half, low_in[k], high_in[k]).astype(f32)
        out[k] = (own + got + added).astype(bf16)


def merge(core, low, high, low_in, high_in, sums, shift):
    half, _, rows, _ = low.shape
    block = min(4, half)
    steps = half // block
    first = lambda i: jnp.minimum(i, steps - 1)
    second = lambda i: jnp.maximum(i - steps, 0)
    return pl.pallas_call(
        merge_kernel,
        grid_spec=pltpu.PrefetchScalarGridSpec(
            num_scalar_prefetch=1,
            grid=(2 * steps,),
            in_specs=[
                pl.BlockSpec((block, 1, rows, D), lambda i, w: (first(i), w[0], 0, 0)),
                pl.BlockSpec((block, 1, rows, D), lambda i, w: (second(i), w[0], 0, 0)),
                pl.BlockSpec((block, rows, D), lambda i, w: (first(i), 0, 0)),
                pl.BlockSpec((block, rows, D), lambda i, w: (second(i), 0, 0)),
                pl.BlockSpec((block,) + sums.shape[1:], lambda i, w: (i, 0, 0)),
                pl.BlockSpec(shift.shape, lambda i, w: (0, 0)),
            ],
            out_specs=pl.BlockSpec((block, rows, D), lambda i, w: (i, 0, 0)),
        ),
        out_shape=jax.ShapeDtypeStruct((2 * half, rows, D), bf16),
        compiler_params=pltpu.CompilerParams(vmem_limit_bytes=60 * MIB),
        name="merge",
    )(jnp.reshape(core, (1,)).astype(jnp.int32), low, high, low_in, high_in, sums, shift)


def place_kernel(where, *refs, pieces, side):
    out, held, sems = refs[-3:]
    kz = 2 * side
    copies = []
    for plane in range(kz):
        for k, (column, places) in enumerate(pieces):
            own, other = refs[2 * k], refs[2 * k + 1]
            rows, cols = own.shape[-2:]
            for index, (z, y, x) in enumerate(places):
                if z != plane:
                    continue
                chip = ((where[0] ^ z) * side + (where[1] ^ y)) * side + (where[2] ^ x)
                if rows % 16 == 0:
                    for ref, core in ((own, where[3]), (other, 1 - where[3])):
                        start = pl.multiple_of((chip * 2 + core) * rows, rows)
                        held[pl.ds(start, rows), pl.ds(column, cols)] = ref[index]
                else:
                    both = [own[index].astype(f32), other[index].astype(f32)]
                    low = jnp.where(where[3] == 0, both[0], both[1])
                    high = jnp.where(where[3] == 0, both[1], both[0])
                    start = pl.multiple_of(chip * 2 * rows, 2 * rows)
                    value = jnp.concatenate([low, high], axis=0).astype(bf16)
                    held[pl.ds(start, 2 * rows), pl.ds(column, cols)] = value
        size = held.shape[0] // kz
        part = pl.ds(pl.multiple_of((where[0] ^ plane) * size, size), size)
        copies.append(pltpu.make_async_copy(held.at[part], out.at[part], sems.at[plane]))
        copies[-1].start()
    for copy in copies:
        copy.wait()


def behind(value, *others):
    return lax.optimization_barrier((value,) + others)[0]


class Net:
    def __init__(self, n):
        chips = n // 2
        side = 1
        while 2 * side * side * side < chips:
            side *= 2
        if 2 * side * side * side != chips:
            raise ValueError("unknown slice")
        self.n, self.side, self.chips = n, side, chips
        self.core = [1]
        self.xy = [2 * k for k in range(1, side * side)]
        self.x = [2 * k for k in range(1, side)]
        self.y = [2 * side * k for k in range(1, side)]
        self.z = [2 * side * side * k for k in range(1, 2 * side)]
        self.me = lax.axis_index("dp")
        self.at_core = self.me % 2
        self.at_xy = (self.me // 2) % (side * side)
        self.at_x = (self.me // 2) % side
        self.at_y = (self.me // (2 * side)) % side
        self.at_z = self.me // (2 * side * side)

    def swap(self, value, offset):
        return lax.ppermute(value, "dp", [(i, i ^ offset) for i in range(self.n)])

    def spread(self, value, offsets):
        return jnp.stack([value] + [self.swap(value, o) for o in offsets])

    def gather_small(self, value, beside=(), chips=False):
        held = value
        order = np.array([0], np.int64)
        steps = []
        for k, offsets in enumerate((self.z, self.xy) if chips else (self.z, self.xy, self.core)):
            held = self.spread(held, offsets)
            if k < len(beside):
                held = behind(held, beside[k])
            steps.append(held)
            order = (np.array([0] + offsets)[:, None] + order[None, :]).reshape(-1)
        return held.reshape((-1,) + value.shape), order, steps

    def plane(self, stacked):
        side = self.side
        places = [(z, 0, 0) for z in range(2 * side)]
        out = [(stacked, places, 0)]
        for k, offset in enumerate(self.xy):
            y, x = divmod(k + 1, side)
            out.append((self.swap(stacked, offset), [(z, y, x) for z, _, _ in places], 0))
        return out

    def place(self, parts, others, after=()):
        side, kz = self.side, 2 * self.side
        rows = parts[0][0].shape[1]
        width = max(column + blocks.shape[2] for blocks, _, column in parts)
        pairs = [(blocks, other) for (blocks, _, _), other in zip(parts, others)]
        shape = (self.n * rows, width)
        if rows % 8 == 0:
            pieces = [(column, places) for _, places, column in parts]
            where = jnp.stack([self.at_z, self.at_y, self.at_x, self.at_core]).astype(jnp.int32)
            inputs = [v for pair in pairs for v in pair]
            return call(
                functools.partial(place_kernel, pieces=pieces, side=side),
                after,
                [smem()] + [pl.BlockSpec(memory_space=pltpu.VMEM)] * len(inputs),
                (where, *inputs),
                vmem=50,
                out_specs=anywhere(),
                out_shape=jax.ShapeDtypeStruct(shape, bf16),
                scratch_shapes=[pltpu.VMEM(shape, bf16), pltpu.SemaphoreType.DMA((kz,))],
                name="place",
            )
        columns = {}
        for (blocks, places, column), pair in zip(parts, pairs):
            columns.setdefault(column, []).extend(
                (core, place, pair[core][k]) for k, place in enumerate(places) for core in (0, 1)
            )
        out = []
        for column in sorted(columns):
            blocks = sorted(columns[column], key=lambda b: (b[1], b[0]))
            held = jnp.stack([b[2] for b in blocks]).reshape(kz, side, side, 2, rows, -1)
            for axis, at in enumerate((self.at_z, self.at_y, self.at_x, self.at_core)):
                held = jnp.take(held, jnp.arange(held.shape[axis]) ^ at, axis=axis)
            out.append(held.reshape(shape[0], -1))
        return jnp.concatenate(out, axis=1)

    def pick(self, value, index, axis):
        return lax.dynamic_index_in_dim(value, index, axis, keepdims=False)

    def start_axis(self, value, axis, at, offsets):
        own = self.pick(value, at, axis)
        return [own] + [
            self.swap(self.pick(value, at ^ (k + 1), axis).astype(bf16), o) for k, o in enumerate(offsets)
        ]

    def finish_axis(self, parts):
        parts = [p.astype(f32) for p in parts]
        while len(parts) > 1:
            parts = [parts[k] + parts[k + 1] for k in range(0, len(parts), 2)]
        return parts[0]

    def scatter_small(self, value):
        kz, k = 2 * self.side, self.side
        value = value.reshape(kz, k * k, 2, -1)
        value = self.finish_axis(self.start_axis(value, 2, self.at_core, self.core)).astype(bf16)
        value = self.finish_axis(self.start_axis(value, 1, self.at_xy, self.xy)).astype(bf16)
        return self.finish_axis(self.start_axis(value, 0, self.at_z, self.z))


def per_device(
    tokens,
    cotangent,
    skip_mask,
    pair_index,
    patch_up,
    patch_down,
    channel_up,
    channel_down,
    patch_upbias,
    patch_downbias,
    first_gain,
    first_shift,
    second_gain,
    second_shift,
    channel_upbias,
    channel_downbias,
    devices,
):
    net = Net(devices)
    chips = devices // 2
    core = net.at_core
    rows = tokens.shape[0]
    crops = rows // S
    unit_d = D // devices
    unit_h = DC // devices
    kz, kxy = 2 * net.side, net.side * net.side

    small = [
        patch_up, patch_down, first_gain, first_shift, second_gain, second_shift, channel_upbias, channel_downbias,
    ]
    sizes = [v.shape[0] for v in small]
    length = sum(sizes)
    padded = -(-length // 1024) * 1024
    packed = join(small, 0, padded)
    every, order, steps = net.gather_small(packed)
    channel_up = behind(channel_up, steps[0])
    skip_mask, pair_index, patch_upbias, patch_downbias = lax.optimization_barrier(
        (skip_mask, pair_index, patch_upbias, patch_downbias, steps[1])
    )[:4]
    in_order = (jnp.arange(devices)[:, None] ^ net.me) == jnp.asarray(order, jnp.int32)[None, :]
    every = dot(in_order.astype(bf16), every).astype(bf16)
    ends = np.cumsum([0] + sizes)
    up_token = every[:, : ends[1]].reshape(S, DS)
    down_token = every[:, ends[1] : ends[2]].reshape(DS, S)
    vecs = every[:, ends[2] : ends[6]].astype(f32).reshape(devices, 4, unit_d).transpose(1, 0, 2).reshape(4, D)
    bias_hidden = every[:, ends[6] : ends[7]].astype(f32).reshape(1, DC)
    bias_out = every[:, ends[7] : ends[8]].astype(f32).reshape(1, D)

    up_stack = net.spread(channel_up.reshape(unit_d, DC), net.z)
    down_stack = net.spread(behind(channel_down, up_stack).reshape(unit_h, D), net.z)
    up_parts = net.plane(up_stack)

    x1, h2, act_t, slope_t, up_pad, down_pad = token_forward(
        skip_mask,
        tokens,
        up_token,
        down_token,
        patch_upbias.astype(f32).reshape(DS, 1),
        patch_downbias.astype(f32).reshape(1, S),
        vecs,
        after=(up_stack, bias_hidden, bias_out),
    )
    up_parts = [(behind(blocks, h2, down_stack), places, column) for blocks, places, column in up_parts]
    up = net.place(up_parts, [net.swap(blocks, 1) for blocks, _, _ in up_parts])
    down_parts = net.plane(behind(down_stack, h2))
    other_pairs, other_skip = net.swap(pair_index, 1), net.swap(skip_mask[:, 1], 1)
    act_low, act_high, z, act_sums = hidden_forward(h2, up, bias_hidden)
    down_parts = [(behind(blocks, act_sums), places, column) for blocks, places, column in down_parts]
    down = net.place(down_parts, [net.swap(blocks, 1) for blocks, _, _ in down_parts])
    outputs, scaled, pooled = output_forward(skip_mask, act_low, act_high, down, x1, bias_out, cotangent)
    other_pairs, other_skip = behind(other_pairs, act_sums), behind(other_skip, act_sums)
    pooled = pooled.reshape(crops, D)

    chip_sums = net.start_axis(act_sums.reshape(crops, chips, 2, unit_h), 2, core, net.core)
    chip_sums = jnp.concatenate([v.astype(bf16).reshape(crops, -1) for v in chip_sums])
    chip_sums = chip_sums.reshape(2 * crops, chips, unit_h).transpose(1, 2, 0)

    def grad_down(act):
        value = lax.dot_general(act, scaled, (((0,), (0,)), ((), ())), preferred_element_type=f32)
        return value.astype(bf16).reshape(chips // 2, 2, unit_h, D)

    low, high = grad_down(act_low), grad_down(act_high)
    every, order, steps = net.gather_small(pooled.astype(bf16), beside=(low, high), chips=True)
    every = every.reshape(-1, D)
    every_other = net.swap(every, 1)
    low, high = behind(low, steps[1]), behind(high, steps[1])
    received = [net.swap(net.pick(v, 1 - core, 1), 1) for v in (low, high)]
    codes = (order[:, None] * crops + np.arange(crops)[None, :]).reshape(1, -1)
    flip = net.me.astype(jnp.int32) * crops

    def find(index):
        code = (index.reshape(-1, 1) ^ flip) - jnp.asarray(codes, jnp.int32)
        return dot((code == 0).astype(bf16), every) + dot((code == crops).astype(bf16), every_other)

    partner = find(jnp.stack([pair_index, other_pairs]))
    differ = pooled - partner[:crops]
    own_code = jnp.stack([net.me, net.me ^ 1]).astype(jnp.int32)[:, None] * crops + jnp.arange(crops, dtype=jnp.int32)
    chip_differ = find(own_code) - partner
    losses = 2.0 * jnp.sum(differ * differ, axis=1)
    differ = differ.reshape(crops // GROUP, GROUP, D)

    chip_keep = jnp.stack([skip_mask[:, 1], other_skip]).astype(f32).reshape(-1, 1) * keep_scale
    chip_shift = (chip_keep * (8.0 / S) * chip_differ).astype(bf16)
    down_sum = merge(core, low, high, *received, chip_sums, chip_shift)
    down_parts = net.start_axis(down_sum.reshape(kz, kxy, unit_h, D), 1, net.at_xy, net.xy)

    gz, up_own, up_other, grad_bias_hidden, grad_bias_out = hidden_backward(
        skip_mask, core, cotangent, differ, h2, down, z, unit_d, after=(down_sum,)
    )
    down_sum = net.finish_axis(down_parts)
    up_other = net.swap(behind(up_other, down_sum), 1)
    down_parts = net.start_axis(down_sum, 0, net.at_z, net.z)
    tiles = rows // TILE
    cuts = (0, 1, tiles - 1, tiles)
    passed = (
        skip_mask, gz, up, x1, cotangent, differ, tokens, act_t, slope_t, down_pad, up_pad, vecs
    )
    done = last_backward(*passed, cuts[0], cuts[1] - cuts[0], after=(down_sum,))
    up_sum = (up_own.astype(f32) + behind(up_other, done[3]).astype(f32)).astype(bf16)
    down_grad = net.finish_axis([behind(v, done[3]) for v in down_parts]).reshape(-1)
    up_parts = net.start_axis(up_sum.reshape(kz, kxy, unit_d, DC), 1, net.at_xy, net.xy)
    done = last_backward(*passed, cuts[1], cuts[2] - cuts[1], before=done, after=(up_sum, down_grad))
    up_sum = net.finish_axis([behind(v, done[3]) for v in up_parts])
    up_parts = net.start_axis(up_sum, 0, net.at_z, net.z)
    grad_tokens, dwd, dwu, sums = last_backward(
        *passed, cuts[2], cuts[3] - cuts[2], before=done, after=(up_sum,)
    )
    up_parts, dwd, dwu, sums = lax.optimization_barrier((up_parts, dwd, dwu, sums))
    up_grad = net.finish_axis(up_parts).reshape(-1)

    grad_patch_up = sum(dwu[c, 4 * c : 4 * c + S] for c in range(GROUP))
    grad_patch_down = sum(dwd[c, :DS, 4 * c : 4 * c + S] for c in range(GROUP))
    bias_up = sum(dwu[c, WIN] for c in range(GROUP))
    bias_down = sum(dwd[c, DS, 4 * c : 4 * c + S] for c in range(GROUP))
    scattered = [
        grad_patch_up, grad_patch_down, sums[0], sums[1], sums[2], sums[3], grad_bias_hidden, grad_bias_out
    ]
    scattered = [v.reshape(devices, -1) for v in scattered]
    scattered += [jnp.broadcast_to(v, (devices,) + v.shape) for v in (bias_up, bias_down)]
    total = sum(v.shape[1] for v in scattered)
    scattered = join([v.astype(bf16) for v in scattered], 1, -(-total // 1024) * 1024)
    own = net.scatter_small(scattered)
    ends = np.cumsum([0] + sizes + [DS, S])
    grads = [own[a:b] for a, b in zip(ends[:-1], ends[1:])]
    return (
        outputs, losses, grad_tokens, grads[0], grads[1], up_grad, down_grad, grads[8], grads[9], *grads[2:8],
    )


def solution(mesh):
    row, flat, whole = P("dp", None), P("dp"), P()
    return jax.shard_map(
        functools.partial(per_device, devices=mesh.shape["dp"]),
        mesh=mesh,
        in_specs=(row, row, row, flat, flat, flat, flat, flat, whole, whole) + (flat,) * 6,
        out_specs=(row, flat, row, flat, flat, flat, flat, whole, whole) + (flat,) * 6,
        check_vma=False,
    )
```

```python
import functools

import jax
import jax.numpy as jnp
import numpy as np
from jax import lax
from jax.experimental import pallas as pl
from jax.experimental.pallas import tpu as pltpu
from jax.sharding import PartitionSpec as P

D = 768
S = 196
DS = 384
DC = 3072

GROUP = 4
TILE = GROUP * S
WIN = 208
STEP = 192
ONES = 16

eps_norm = 1e-06
keep_scale = 4.0 / 3.0
f32 = jnp.float32
bf16 = jnp.bfloat16
MIB = 1024 * 1024


def resident(shape):
    zeros = (0,) * len(shape)
    return pl.BlockSpec(shape, lambda *_: zeros, pipeline_mode=pl.Buffered(1))


def smem():
    return pl.BlockSpec(memory_space=pltpu.SMEM)


def anywhere():
    return pl.BlockSpec(memory_space=pl.ANY)


def call(kernel, after, in_specs, args, vmem, **rest):
    count = len(args)

    def body(*refs):
        kernel(*refs[:count], *refs[count + len(after) :])

    return pl.pallas_call(
        body,
        in_specs=list(in_specs) + [anywhere()] * len(after),
        compiler_params=pltpu.CompilerParams(vmem_limit_bytes=vmem * MIB),
        **rest,
    )(*args, *after)


def kept(skip, crop, branch):
    return skip[crop, branch].astype(f32) * keep_scale


def dot(a, b):
    return jnp.dot(a, b, preferred_element_type=f32)


def dot_nt(a, b):
    return lax.dot_general(a, b, (((1,), (1,)), ((), ())), preferred_element_type=f32)


def gelu_and_slope(z):
    phi = 0.5 * (1.0 + lax.erf(z * 0.7071067811865476))
    return z * phi, phi + z * jnp.exp(-0.5 * z * z) * 0.3989422804014327


def normalize(v):
    center = v - jnp.mean(v, axis=-1, keepdims=True)
    inv = lax.rsqrt(jnp.mean(center * center, axis=-1, keepdims=True) + eps_norm)
    return center * inv, inv


def join(values, axis, total):
    out, start = None, 0
    for v in values:
        pads = [(0, 0)] * v.ndim
        pads[axis] = (start, total - start - v.shape[axis])
        start += v.shape[axis]
        v = jnp.pad(v, pads)
        out = v if out is None else out + v
    return out


def per_row(values, shape, start=0):
    rows = lax.broadcasted_iota(jnp.int32, shape, 0) + start
    out = jnp.broadcast_to(values[GROUP - 1], shape)
    for c in range(GROUP - 2, -1, -1):
        out = jnp.where(rows < (c + 1) * S, values[c], out)
    return out


def crop_sum(read, c):
    lo, hi = c * S, (c + 1) * S
    base = c * STEP
    width = read(base, 8).shape[1]
    total = jnp.sum(read(base + 16, STEP - 16), axis=0, keepdims=True)
    for piece in (base, base + STEP):
        rows = lax.broadcasted_iota(jnp.int32, (16, width), 0) + piece
        ok = (rows >= lo) & (rows < hi)
        total += jnp.sum(jnp.where(ok, read(piece, 16), 0.0), axis=0, keepdims=True)
    return total


def window_matrix(c, shape):
    return jnp.where(
        lax.broadcasted_iota(jnp.int32, shape, 0) == lax.broadcasted_iota(jnp.int32, shape, 1) + 4 * c, 1.0, 0.0
    ).astype(bf16)


def token_forward_kernel(skip, x, wu, wd, bu, bd, vecs, x1_out, h2, act, slope, wu_out, wd_out, h1, x1, wut, wdt, bdt):
    i = pl.program_id(0)

    @pl.when(i == 0)
    def _():
        for c in range(GROUP):
            move = window_matrix(c, (WIN, S))
            wu_out[c] = dot(move, wu[...]).astype(bf16)
            wut[c] = lax.dot_general(
                wu[...], move, (((0,), (1,)), ((), ())), preferred_element_type=f32
            ).astype(bf16)
            wd_out[c] = dot_nt(wd[...], move).astype(bf16)
            wdt[c] = dot_nt(move, wd[...]).astype(bf16)
            bdt[c] = jnp.sum(move.astype(f32) * bd[...], axis=1, keepdims=True)

    tokens = x[...].astype(f32)
    normed, _ = normalize(tokens)
    h1[...] = (normed * vecs[0:1, :] + vecs[1:2, :]).astype(bf16)
    x1[...] = tokens

    def lift(c):
        return dot(wut[c], h1[pl.ds(c * STEP, WIN), :]) + bu[...]

    later = lift(0)
    for c in range(GROUP):
        lifted, later = later, lift(c + 1) if c + 1 < GROUP else None
        value, grad = gelu_and_slope(lifted)
        value = value.astype(bf16)
        act[c] = value
        slope[c] = grad.astype(bf16)
        mixed = dot(wdt[c], value) + bdt[c]
        x1[pl.ds(c * STEP, WIN), :] += kept(skip, i * GROUP + c, 0) * mixed
    x1_out[...] = x1[...].astype(bf16)
    normed, _ = normalize(x1[...])
    h2[...] = (normed * vecs[2:3, :] + vecs[3:4, :]).astype(bf16)


def token_forward(skip, x, wu, wd, bu, bd, vecs, after=()):
    rows = x.shape[0]
    crops = rows // S
    tile = pl.BlockSpec((TILE, D), lambda i: (i, 0))
    hidden = pl.BlockSpec((GROUP, DS, D), lambda i: (i, 0, 0))
    moved = [(GROUP, WIN, DS), (GROUP, DS, WIN)]
    return call(
        token_forward_kernel,
        after,
        [
            smem(),
            tile,
            resident((S, DS)),
            resident((DS, S)),
            resident((DS, 1)),
            resident((1, S)),
            resident((4, D)),
        ],
        (skip, x, wu, wd, bu, bd, vecs),
        vmem=50,
        grid=(rows // TILE,),
        out_specs=[tile, tile, hidden, hidden] + [pl.BlockSpec(m, lambda i: (0, 0, 0)) for m in moved],
        out_shape=[
            jax.ShapeDtypeStruct((rows, D), bf16),
            jax.ShapeDtypeStruct((rows, D), bf16),
            jax.ShapeDtypeStruct((crops, DS, D), bf16),
            jax.ShapeDtypeStruct((crops, DS, D), bf16),
        ]
        + [jax.ShapeDtypeStruct(m, bf16) for m in moved],
        scratch_shapes=[
            pltpu.VMEM((TILE, D), bf16),
            pltpu.VMEM((TILE, D), f32),
            pltpu.VMEM((GROUP, DS, WIN), bf16),
            pltpu.VMEM((GROUP, WIN, DS), bf16),
            pltpu.VMEM((GROUP, WIN, 1), f32),
        ],
        cost_estimate=pl.CostEstimate(
            flops=20 * rows * DS * D, bytes_accessed=rows * D * 12, transcendentals=0
        ),
        name="token_forward",
    )


def hidden_kernel(h2, up, bias, act_low, act_high, z_out, sums):
    i = pl.program_id(0)
    chunk = 512
    count = DC // chunk

    def hidden(j):
        cols = pl.ds(j * chunk, chunk)
        return dot(h2[...], up[:, cols]) + bias[:, cols]

    later = hidden(0)
    for j in range(count):
        cols = pl.ds(j * chunk, chunk)
        z, later = later, hidden(j + 1) if j + 1 < count else None
        z_out[:, cols] = z.astype(bf16)
        value = z * (0.5 * (1.0 + lax.erf(z * 0.7071067811865476)))
        half, k = divmod(j, count // 2)
        (act_low, act_high)[half][:, pl.ds(k * chunk, chunk)] = value.astype(bf16)
        for c in range(GROUP):
            sums[pl.ds(i * GROUP + c, 1), cols] = crop_sum(lambda a, n: value[a : a + n], c)


def hidden_forward(h2, up, bias, after=()):
    rows = h2.shape[0]
    grid = rows // TILE
    half = pl.BlockSpec((TILE, DC // 2), lambda i: (i, 0))
    return call(
        hidden_kernel,
        after,
        [pl.BlockSpec((TILE, D), lambda i: (i, 0)), resident((D, DC)), resident((1, DC))],
        (h2, up, bias),
        vmem=60,
        grid=(grid,),
        out_specs=[
            half,
            half,
            pl.BlockSpec((TILE, DC), lambda i: (i, 0)),
            pl.BlockSpec((grid * GROUP, DC), lambda i: (0, 0)),
        ],
        out_shape=[
            jax.ShapeDtypeStruct((rows, DC // 2), bf16),
            jax.ShapeDtypeStruct((rows, DC // 2), bf16),
            jax.ShapeDtypeStruct((rows, DC), bf16),
            jax.ShapeDtypeStruct((grid * GROUP, DC), f32),
        ],
        cost_estimate=pl.CostEstimate(
            flops=3 * rows * D * DC, bytes_accessed=rows * DC * 4, transcendentals=0
        ),
        name="hidden_forward",
    )


def output_kernel(skip, act_low, act_high, down, x1, bias, cotangent, out, scaled, pooled):
    i = pl.program_id(0)
    scale = per_row([kept(skip, i * GROUP + c, 1) for c in range(GROUP)], (TILE, 1))
    branch = dot(act_low[...], down[pl.ds(0, DC // 2), :]) + bias[...]
    branch += dot(act_high[...], down[pl.ds(DC // 2, DC // 2), :])
    y = x1[...].astype(f32) + scale * branch
    out[...] = y.astype(bf16)
    scaled[...] = (scale * cotangent[...].astype(f32)).astype(bf16)
    for c in range(GROUP):
        pooled[pl.ds(i * GROUP + c, 1), :] = crop_sum(lambda a, n: y[a : a + n], c) * (1.0 / S)


def output_forward(skip, act_low, act_high, down, x1, bias, cotangent, after=()):
    rows = x1.shape[0]
    grid = rows // TILE
    tile = pl.BlockSpec((TILE, D), lambda i: (i, 0))
    half = pl.BlockSpec((TILE, DC // 2), lambda i: (i, 0))
    return call(
        output_kernel,
        after,
        [smem(), half, half, resident((DC, D)), tile, resident((1, D)), tile],
        (skip, act_low, act_high, down, x1, bias, cotangent),
        vmem=60,
        grid=(grid,),
        out_specs=[tile, tile, pl.BlockSpec((grid * GROUP, D), lambda i: (0, 0))],
        out_shape=[
            jax.ShapeDtypeStruct((rows, D), bf16),
            jax.ShapeDtypeStruct((rows, D), bf16),
            jax.ShapeDtypeStruct((grid * GROUP, D), f32),
        ],
        cost_estimate=pl.CostEstimate(
            flops=2 * rows * D * DC, bytes_accessed=rows * DC * 2 + rows * D * 10, transcendentals=0
        ),
        name="output_forward",
    )


def lane_blocks(rows):
    count = max(rows // 768, 1)
    return [(k * 768, 768 if k < count - 1 else rows - 768 * (count - 1)) for k in range(count)]


def hidden_backward_kernel(
    skip, where, cotangent, differ, h2, down, z, gz, dw_own, dw_other, db, sums, grad, h2t
):
    j = pl.program_id(0)
    blocks = lane_blocks(h2.shape[0])

    @pl.when(j == 0)
    def _():
        total = jnp.zeros((1, D), f32)
        for i in range(cotangent.shape[0] // TILE):
            rows = pl.ds(i * TILE, TILE)
            scale = per_row([kept(skip, i * GROUP + c, 1) for c in range(GROUP)], (TILE, 1))
            shift = per_row([differ[pl.ds(i * GROUP + c, 1), :] for c in range(GROUP)], (TILE, D))
            value = (scale * (cotangent[rows, :].astype(f32) + (8.0 / S) * shift)).astype(bf16)
            grad[rows, :] = value
            total += jnp.sum(value.astype(f32), axis=0, keepdims=True)
        sums[...] = total
        square = (D, D)
        same = lax.broadcasted_iota(jnp.int32, square, 0) == lax.broadcasted_iota(jnp.int32, square, 1)
        eye = jnp.where(same, 1.0, 0.0).astype(bf16)
        for start, size in blocks:
            h2t[:, pl.ds(start, size)] = dot_nt(eye, h2[pl.ds(start, size), :]).astype(bf16)

    def first(b):
        start, size = blocks[b]
        return dot_nt(grad[pl.ds(start, size), :], down[...])

    dw = db_sum = None
    later = first(0)
    for b, (start, size) in enumerate(blocks):
        rows = pl.ds(start, size)
        part, later = later, first(b + 1) if b + 1 < len(blocks) else None
        hidden = z[rows, :].astype(f32)
        slope = (
            0.5 * (1.0 + lax.erf(hidden * 0.7071067811865476))
            + hidden * jnp.exp(-0.5 * hidden * hidden) * 0.3989422804014327
        )
        part = part * slope
        added = jnp.sum(part, axis=0, keepdims=True)
        db_sum = added if db_sum is None else db_sum + added
        part = part.astype(bf16)
        gz[rows, :] = part
        added = dot(h2t[:, rows], part)
        dw = added if dw is None else dw + added
    db[...] = db_sum
    unit = dw_own.shape[1]
    dw = dw.reshape(D // (2 * unit), 2, unit, dw.shape[1])
    dw_own[...] = jnp.where(where[0] == 0, dw[:, 0], dw[:, 1]).astype(bf16)
    dw_other[...] = jnp.where(where[0] == 0, dw[:, 1], dw[:, 0]).astype(bf16)


def hidden_backward(skip, core, cotangent, differ, h2, down, z, unit, after=()):
    rows = cotangent.shape[0]
    chunk = 512
    grads = (D // (2 * unit), unit)
    wide = pl.BlockSpec((rows, chunk), lambda j: (0, j))
    return call(
        hidden_backward_kernel,
        after,
        [
            smem(),
            smem(),
            resident((rows, D)),
            resident(differ.shape),
            resident((rows, D)),
            pl.BlockSpec((chunk, D), lambda j: (j, 0)),
            wide,
        ],
        (skip, jnp.reshape(core, (1,)).astype(jnp.int32), cotangent, differ, h2, down, z),
        vmem=52,
        grid=(DC // chunk,),
        out_specs=[
            wide,
            pl.BlockSpec(grads + (chunk,), lambda j: (0, 0, j)),
            pl.BlockSpec(grads + (chunk,), lambda j: (0, 0, j)),
            pl.BlockSpec((1, chunk), lambda j: (0, j)),
            pl.BlockSpec((1, D), lambda j: (0, 0)),
        ],
        out_shape=[
            jax.ShapeDtypeStruct((rows, DC), bf16),
            jax.ShapeDtypeStruct(grads + (DC,), bf16),
            jax.ShapeDtypeStruct(grads + (DC,), bf16),
            jax.ShapeDtypeStruct((1, DC), f32),
            jax.ShapeDtypeStruct((1, D), f32),
        ],
        scratch_shapes=[pltpu.VMEM((rows, D), bf16), pltpu.VMEM((D, rows), bf16)],
        cost_estimate=pl.CostEstimate(
            flops=4 * rows * D * DC, bytes_accessed=rows * DC * 4, transcendentals=0
        ),
        name="hidden_backward",
    )


def norm_back(grad, gain, normed, inv):
    scaled = grad * gain
    return inv * (
        scaled
        - jnp.mean(scaled, axis=-1, keepdims=True)
        - normed * jnp.mean(scaled * normed, axis=-1, keepdims=True)
    )


def last_backward_kernel(
    skip, gz, up, x1, cotangent, differ, x, act, slope, wd, wu, vecs, *rest, begin, first
):
    start, (out, dwd, dwu, sums, gh2, gx1, gv, h1, gh1) = rest[:-9], rest[-9:]
    i = pl.program_id(0)

    @pl.when(i == 0)
    def _():
        if first:
            dwd[...] = jnp.zeros_like(dwd)
            dwu[...] = jnp.zeros_like(dwu)
            sums[...] = jnp.zeros_like(sums)
        else:
            dwd[...] = start[1][...]
            dwu[...] = start[2][...]
            sums[...] = start[3][...]

    i += begin

    def add(row, value):
        sums[row : row + 1, :] += jnp.sum(value, axis=0, keepdims=True)

    block = TILE // 2
    for p in range(2):
        rows = pl.ds(p * block, block)
        gh2[rows, :] = dot_nt(gz[rows, :], up[...])
    normed_one, inv_one = normalize(x[...].astype(f32))
    h1[...] = (normed_one * vecs[0:1, :] + vecs[1:2, :]).astype(bf16)
    for p in range(2):
        rows = pl.ds(p * block, block)
        grad = gh2[rows, :]
        normed, inv = normalize(x1[rows, :].astype(f32))
        add(2, grad * normed)
        add(3, grad)
        shift = per_row(
            [differ[pl.ds(i * GROUP + c, 1), :] for c in range(GROUP)], (block, D), start=p * block
        )
        value = (
            cotangent[rows, :].astype(f32)
            + (8.0 / S) * shift
            + norm_back(grad, vecs[2:3, :], normed, inv)
        )
        gx1[rows, :] = value
        scale = per_row(
            [kept(skip, i * GROUP + c, 0) for c in range(GROUP)], (block, 1), start=p * block
        )
        gv[rows, :] = (scale * value).astype(bf16)

    gh1[...] = jnp.zeros_like(gh1)
    ones = jnp.ones((ONES, D), bf16)

    def back(c):
        return dot(wd[c], gv[pl.ds(c * STEP, WIN), :])

    later = back(0)
    for c in range(GROUP):
        rows = pl.ds(c * STEP, WIN)
        grad, later = later, back(c + 1) if c + 1 < GROUP else None
        dwd[c] += dot_nt(jnp.concatenate([act[c], ones], axis=0), gv[rows, :])
        gu = (grad * slope[c].astype(f32)).astype(bf16)
        dwu[c] += dot_nt(jnp.concatenate([h1[rows, :], ones], axis=0), gu)
        gh1[rows, :] += dot(wu[c], gu)
    grad = gh1[...]
    add(0, grad * normed_one)
    add(1, grad)
    out[...] = gx1[...] + norm_back(grad, vecs[0:1, :], normed_one, inv_one)


def last_backward(
    skip, gz, up, x1, cotangent, differ, x, act, slope, wd, wu, vecs, begin, count, before=None, after=()
):
    rows = x.shape[0]
    tile = pl.BlockSpec((TILE, D), lambda i: (i + begin, 0))
    hidden = pl.BlockSpec((GROUP, DS, D), lambda i: (i + begin, 0, 0))
    shapes = [(GROUP, DS + ONES, WIN), (GROUP, WIN + ONES, DS), (4, D)]
    extra = () if before is None else tuple(before)
    return call(
        functools.partial(last_backward_kernel, begin=begin, first=before is None),
        after,
        [
            smem(),
            pl.BlockSpec((TILE, DC), lambda i: (i + begin, 0)),
            resident((D, DC)),
            tile,
            tile,
            resident(differ.shape),
            tile,
            hidden,
            hidden,
            resident((GROUP, DS, WIN)),
            resident((GROUP, WIN, DS)),
            resident((4, D)),
        ]
        + ([] if before is None else [anywhere()] + [resident(s) for s in shapes]),
        (skip, gz, up, x1, cotangent, differ, x, act, slope, wd, wu, vecs) + extra,
        vmem=48,
        grid=(count,),
        out_specs=[
            tile,
            pl.BlockSpec(shapes[0], lambda i: (0, 0, 0)),
            pl.BlockSpec(shapes[1], lambda i: (0, 0, 0)),
            pl.BlockSpec(shapes[2], lambda i: (0, 0)),
        ],
        out_shape=[jax.ShapeDtypeStruct((rows, D), f32)] + [jax.ShapeDtypeStruct(s, f32) for s in shapes],
        scratch_shapes=[
            pltpu.VMEM((TILE, D), f32),
            pltpu.VMEM((TILE, D), f32),
            pltpu.VMEM((TILE, D), bf16),
            pltpu.VMEM((TILE, D), bf16),
            pltpu.VMEM((TILE, D), f32),
        ],
        input_output_aliases={} if before is None else {12: 0},
        cost_estimate=pl.CostEstimate(
            flops=count * TILE * (2 * D * DC + 20 * DS * D),
            bytes_accessed=count * TILE * (DC * 2 + D * 24),
            transcendentals=0,
        ),
        name="last_backward",
    )


def merge_kernel(where, low, high, low_in, high_in, sums, shift, *outs):
    i = pl.program_id(0)
    half = pl.num_programs(0) // 2
    *outs, over = outs
    over[...] = jnp.zeros_like(over)
    for k, out in enumerate(outs):
        place = where[1] ^ k
        added = dot(sums[place, 0], shift[...])
        own = jnp.where(i < half, low[place, 0], high[place, 0]).astype(f32)
        got = jnp.where(i < half, low_in[place], high_in[place]).astype(f32)
        out[0] = (own + got + added).astype(bf16)


def merge(core, at_xy, plane, low, high, low_in, high_in, sums, shift):
    half, _, rows, _ = low.shape
    steps = half // plane
    first = lambda i: jnp.minimum(i, steps - 1)
    second = lambda i: jnp.maximum(i - steps, 0)
    return pl.pallas_call(
        merge_kernel,
        grid_spec=pltpu.PrefetchScalarGridSpec(
            num_scalar_prefetch=1,
            grid=(2 * steps,),
            in_specs=[
                pl.BlockSpec((plane, 1, rows, D), lambda i, w: (first(i), w[0], 0, 0)),
                pl.BlockSpec((plane, 1, rows, D), lambda i, w: (second(i), w[0], 0, 0)),
                pl.BlockSpec((plane, rows, D), lambda i, w: (first(i), 0, 0)),
                pl.BlockSpec((plane, rows, D), lambda i, w: (second(i), 0, 0)),
                pl.BlockSpec((plane, 1) + sums.shape[2:], lambda i, w: (i, w[0], 0, 0)),
                pl.BlockSpec(shift.shape, lambda i, w: (0, 0)),
            ],
            out_specs=[pl.BlockSpec((1, rows, D), lambda i, w: (i, 0, 0))] * plane
            + [pl.BlockSpec((8, 128), lambda i, w: (0, 0))],
        ),
        out_shape=[jax.ShapeDtypeStruct((2 * steps, rows, D), bf16)] * plane
        + [jax.ShapeDtypeStruct((8, 128), f32)],
        compiler_params=pltpu.CompilerParams(vmem_limit_bytes=60 * MIB),
        name="merge",
    )(jnp.stack([core, at_xy]).astype(jnp.int32), low, high, low_in, high_in, sums, shift)


def place_kernel(where, *refs, pieces, side):
    out, held, sems = refs[-3:]
    kz = 2 * side
    copies = []
    for plane in range(kz):
        for k, (column, places) in enumerate(pieces):
            own, other = refs[2 * k], refs[2 * k + 1]
            rows, cols = own.shape[-2:]
            for index, (z, y, x) in enumerate(places):
                if z != plane:
                    continue
                chip = ((where[0] ^ z) * side + (where[1] ^ y)) * side + (where[2] ^ x)
                if rows % 16 == 0:
                    for ref, core in ((own, where[3]), (other, 1 - where[3])):
                        start = pl.multiple_of((chip * 2 + core) * rows, rows)
                        held[pl.ds(start, rows), pl.ds(column, cols)] = ref[index]
                else:
                    both = [own[index].astype(f32), other[index].astype(f32)]
                    low = jnp.where(where[3] == 0, both[0], both[1])
                    high = jnp.where(where[3] == 0, both[1], both[0])
                    start = pl.multiple_of(chip * 2 * rows, 2 * rows)
                    value = jnp.concatenate([low, high], axis=0).astype(bf16)
                    held[pl.ds(start, 2 * rows), pl.ds(column, cols)] = value
        size = held.shape[0] // kz
        part = pl.ds(pl.multiple_of((where[0] ^ plane) * size, size), size)
        copies.append(pltpu.make_async_copy(held.at[part], out.at[part], sems.at[plane]))
        copies[-1].start()
    for copy in copies:
        copy.wait()


def behind(value, *others):
    return lax.optimization_barrier((value,) + others)[0]


class Net:
    def __init__(self, n):
        chips = n // 2
        side = 1
        while 2 * side * side * side < chips:
            side *= 2
        if 2 * side * side * side != chips:
            raise ValueError("unknown slice")
        self.n, self.side, self.chips = n, side, chips
        self.core = [1]
        self.xy = [2 * k for k in range(1, side * side)]
        self.x = [2 * k for k in range(1, side)]
        self.y = [2 * side * k for k in range(1, side)]
        self.z = [2 * side * side * k for k in range(1, 2 * side)]
        self.me = lax.axis_index("dp")
        self.at_core = self.me % 2
        self.at_xy = (self.me // 2) % (side * side)
        self.at_x = (self.me // 2) % side
        self.at_y = (self.me // (2 * side)) % side
        self.at_z = self.me // (2 * side * side)

    def swap(self, value, offset):
        return lax.ppermute(value, "dp", [(i, i ^ offset) for i in range(self.n)])

    def spread(self, value, offsets):
        return jnp.stack([value] + [self.swap(value, o) for o in offsets])

    def gather_small(self, value, beside=(), chips=False):
        held = value
        order = np.array([0], np.int64)
        steps = []
        for k, offsets in enumerate((self.z, self.xy) if chips else (self.z, self.xy, self.core)):
            held = self.spread(held, offsets)
            if k < len(beside):
                held = behind(held, beside[k])
            steps.append(held)
            order = (np.array([0] + offsets)[:, None] + order[None, :]).reshape(-1)
        return held.reshape((-1,) + value.shape), order, steps

    def plane(self, stacked):
        side = self.side
        places = [(z, 0, 0) for z in range(2 * side)]
        out = [(stacked, places, 0)]
        for k, offset in enumerate(self.xy):
            y, x = divmod(k + 1, side)
            out.append((self.swap(stacked, offset), [(z, y, x) for z, _, _ in places], 0))
        return out

    def place(self, parts, others, after=()):
        side, kz = self.side, 2 * self.side
        rows = parts[0][0].shape[1]
        width = max(column + blocks.shape[2] for blocks, _, column in parts)
        pairs = [(blocks, other) for (blocks, _, _), other in zip(parts, others)]
        shape = (self.n * rows, width)
        if rows % 8 == 0:
            pieces = [(column, places) for _, places, column in parts]
            where = jnp.stack([self.at_z, self.at_y, self.at_x, self.at_core]).astype(jnp.int32)
            inputs = [v for pair in pairs for v in pair]
            return call(
                functools.partial(place_kernel, pieces=pieces, side=side),
                after,
                [smem()] + [pl.BlockSpec(memory_space=pltpu.VMEM)] * len(inputs),
                (where, *inputs),
                vmem=50,
                out_specs=anywhere(),
                out_shape=jax.ShapeDtypeStruct(shape, bf16),
                scratch_shapes=[pltpu.VMEM(shape, bf16), pltpu.SemaphoreType.DMA((kz,))],
                name="place",
            )
        columns = {}
        for (blocks, places, column), pair in zip(parts, pairs):
            columns.setdefault(column, []).extend(
                (core, place, pair[core][k]) for k, place in enumerate(places) for core in (0, 1)
            )
        out = []
        for column in sorted(columns):
            blocks = sorted(columns[column], key=lambda b: (b[1], b[0]))
            held = jnp.stack([b[2] for b in blocks]).reshape(kz, side, side, 2, rows, -1)
            for axis, at in enumerate((self.at_z, self.at_y, self.at_x, self.at_core)):
                held = jnp.take(held, jnp.arange(held.shape[axis]) ^ at, axis=axis)
            out.append(held.reshape(shape[0], -1))
        return jnp.concatenate(out, axis=1)

    def pick(self, value, index, axis):
        return lax.dynamic_index_in_dim(value, index, axis, keepdims=False)

    def start_axis(self, value, axis, at, offsets):
        own = self.pick(value, at, axis)
        return [own] + [
            self.swap(self.pick(value, at ^ (k + 1), axis).astype(bf16), o) for k, o in enumerate(offsets)
        ]

    def finish_axis(self, parts):
        parts = [p.astype(f32) for p in parts]
        while len(parts) > 1:
            parts = [parts[k] + parts[k + 1] for k in range(0, len(parts), 2)]
        return parts[0]

    def scatter_small(self, value):
        kz, k = 2 * self.side, self.side
        value = value.reshape(kz, k * k, 2, -1)
        value = self.finish_axis(self.start_axis(value, 2, self.at_core, self.core)).astype(bf16)
        value = self.finish_axis(self.start_axis(value, 1, self.at_xy, self.xy)).astype(bf16)
        return self.finish_axis(self.start_axis(value, 0, self.at_z, self.z))


def per_device(
    tokens,
    cotangent,
    skip_mask,
    pair_index,
    patch_up,
    patch_down,
    channel_up,
    channel_down,
    patch_upbias,
    patch_downbias,
    first_gain,
    first_shift,
    second_gain,
    second_shift,
    channel_upbias,
    channel_downbias,
    devices,
):
    net = Net(devices)
    chips = devices // 2
    core = net.at_core
    rows = tokens.shape[0]
    crops = rows // S
    unit_d = D // devices
    unit_h = DC // devices
    kz, kxy = 2 * net.side, net.side * net.side

    small = [
        patch_up, patch_down, first_gain, first_shift, second_gain, second_shift, channel_upbias, channel_downbias,
    ]
    sizes = [v.shape[0] for v in small]
    length = sum(sizes)
    padded = -(-length // 1024) * 1024
    packed = join(small, 0, padded)
    every, order, steps = net.gather_small(packed)
    channel_up = behind(channel_up, steps[0])
    skip_mask, pair_index, patch_upbias, patch_downbias = lax.optimization_barrier(
        (skip_mask, pair_index, patch_upbias, patch_downbias, steps[1])
    )[:4]
    in_order = (jnp.arange(devices)[:, None] ^ net.me) == jnp.asarray(order, jnp.int32)[None, :]
    every = dot(in_order.astype(bf16), every).astype(bf16)
    ends = np.cumsum([0] + sizes)
    up_token = every[:, : ends[1]].reshape(S, DS)
    down_token = every[:, ends[1] : ends[2]].reshape(DS, S)
    vecs = every[:, ends[2] : ends[6]].astype(f32).reshape(devices, 4, unit_d).transpose(1, 0, 2).reshape(4, D)
    bias_hidden = every[:, ends[6] : ends[7]].astype(f32).reshape(1, DC)
    bias_out = every[:, ends[7] : ends[8]].astype(f32).reshape(1, D)

    up_stack = net.spread(channel_up.reshape(unit_d, DC), net.z)
    down_stack = net.spread(behind(channel_down, up_stack).reshape(unit_h, D), net.z)
    up_parts = net.plane(up_stack)

    x1, h2, act_t, slope_t, up_pad, down_pad = token_forward(
        skip_mask,
        tokens,
        up_token,
        down_token,
        patch_upbias.astype(f32).reshape(DS, 1),
        patch_downbias.astype(f32).reshape(1, S),
        vecs,
        after=(up_stack, bias_hidden, bias_out),
    )
    up_parts = [(behind(blocks, h2, down_stack), places, column) for blocks, places, column in up_parts]
    up = net.place(up_parts, [net.swap(blocks, 1) for blocks, _, _ in up_parts])
    down_parts = net.plane(behind(down_stack, h2))
    other_pairs, other_skip = net.swap(pair_index, 1), net.swap(skip_mask[:, 1], 1)
    act_low, act_high, z, act_sums = hidden_forward(h2, up, bias_hidden)
    down_parts = [(behind(blocks, act_sums), places, column) for blocks, places, column in down_parts]
    down = net.place(down_parts, [net.swap(blocks, 1) for blocks, _, _ in down_parts])
    outputs, scaled, pooled = output_forward(skip_mask, act_low, act_high, down, x1, bias_out, cotangent)
    other_pairs, other_skip = behind(other_pairs, act_sums), behind(other_skip, act_sums)

    chip_sums = act_sums.astype(bf16)
    chip_sums = jnp.concatenate([chip_sums, net.swap(chip_sums, 1)]).T.reshape(chips, 2, unit_h, 2 * crops)

    def grad_down(act):
        value = lax.dot_general(act, scaled, (((0,), (0,)), ((), ())), preferred_element_type=f32)
        return value.astype(bf16).reshape(chips // 2, 2, unit_h, D)

    low, high = grad_down(act_low), grad_down(act_high)
    every, order, steps = net.gather_small(pooled.astype(bf16), beside=(low, high), chips=True)
    every = every.reshape(-1, D)
    every_other = net.swap(every, 1)
    low, high = behind(low, steps[1]), behind(high, steps[1])
    received = [net.swap(net.pick(v, 1 - core, 1), 1) for v in (low, high)]
    codes = (order[:, None] * crops + np.arange(crops)[None, :]).reshape(1, -1)
    flip = net.me.astype(jnp.int32) * crops

    def find(index):
        code = (index.reshape(-1, 1) ^ flip) - jnp.asarray(codes, jnp.int32)
        return dot((code == 0).astype(bf16), every) + dot((code == crops).astype(bf16), every_other)

    partner = find(jnp.stack([pair_index, other_pairs]))
    differ = pooled - partner[:crops]
    own_code = jnp.stack([net.me, net.me ^ 1]).astype(jnp.int32)[:, None] * crops + jnp.arange(crops, dtype=jnp.int32)
    chip_differ = find(own_code) - partner
    losses = 2.0 * jnp.sum(differ * differ, axis=1)

    chip_keep = jnp.stack([skip_mask[:, 1], other_skip]).astype(f32).reshape(-1, 1) * keep_scale
    chip_shift = (chip_keep * (8.0 / S) * chip_differ).astype(bf16)
    *down_sum, over = merge(core, net.at_xy, kxy, low, high, *received, chip_sums, chip_shift)
    down_parts = [down_sum[0]] + [net.swap(v, o) for v, o in zip(down_sum[1:], net.xy)]

    gz, up_own, up_other, grad_bias_hidden, grad_bias_out = hidden_backward(
        skip_mask, core, cotangent, differ, h2, down, z, unit_d, after=(over,)
    )
    down_sum = net.finish_axis(down_parts)
    up_other = net.swap(behind(up_other, down_sum), 1)
    down_parts = net.start_axis(down_sum, 0, net.at_z, net.z)
    tiles = rows // TILE
    cuts = (0, 1, tiles)
    passed = (
        skip_mask, gz, up, x1, cotangent, differ, tokens, act_t, slope_t, down_pad, up_pad, vecs
    )
    done = last_backward(*passed, cuts[0], cuts[1] - cuts[0], after=(down_sum,))
    up_sum = (up_own.astype(f32) + behind(up_other, done[3]).astype(f32)).astype(bf16)
    down_grad = net.finish_axis([behind(v, done[3]) for v in down_parts]).reshape(-1)
    up_parts = net.start_axis(up_sum.reshape(kz, kxy, unit_d, DC), 1, net.at_xy, net.xy)
    grad_tokens, dwd, dwu, sums = last_backward(
        *passed, cuts[1], cuts[2] - cuts[1], before=done, after=(up_sum, down_grad)
    )
    up_sum = net.finish_axis([behind(v, sums) for v in up_parts])
    dwd, dwu, sums, up_sum = lax.optimization_barrier((dwd, dwu, sums, up_sum))
    up_parts = net.start_axis(up_sum, 0, net.at_z, net.z)
    up_grad = net.finish_axis(up_parts).reshape(-1)

    grad_patch_up = sum(dwu[c, 4 * c : 4 * c + S] for c in range(GROUP))
    grad_patch_down = sum(dwd[c, :DS, 4 * c : 4 * c + S] for c in range(GROUP))
    bias_up = sum(dwu[c, WIN] for c in range(GROUP))
    bias_down = sum(dwd[c, DS, 4 * c : 4 * c + S] for c in range(GROUP))
    scattered = [
        grad_patch_up, grad_patch_down, sums[0], sums[1], sums[2], sums[3], grad_bias_hidden, grad_bias_out
    ]
    scattered = [v.reshape(devices, -1) for v in scattered]
    scattered += [jnp.broadcast_to(v, (devices,) + v.shape) for v in (bias_up, bias_down)]
    total = sum(v.shape[1] for v in scattered)
    scattered = join([v.astype(bf16) for v in scattered], 1, -(-total // 1024) * 1024)
    own = net.scatter_small(scattered)
    ends = np.cumsum([0] + sizes + [DS, S])
    grads = [own[a:b] for a, b in zip(ends[:-1], ends[1:])]
    return (
        outputs, losses, grad_tokens, grads[0], grads[1], up_grad, down_grad, grads[8], grads[9], *grads[2:8],
    )


def solution(mesh):
    row, flat, whole = P("dp", None), P("dp"), P()
    return jax.shard_map(
        functools.partial(per_device, devices=mesh.shape["dp"]),
        mesh=mesh,
        in_specs=(row, row, row, flat, flat, flat, flat, flat, whole, whole) + (flat,) * 6,
        out_specs=(row, flat, row, flat, flat, flat, flat, whole, whole) + (flat,) * 6,
        check_vma=False,
    )
```

```python
import functools

import jax
import jax.numpy as jnp
import numpy as np
from jax import lax
from jax.experimental import pallas as pl
from jax.experimental.pallas import tpu as pltpu
from jax.sharding import PartitionSpec as P

D = 768
S = 196
DS = 384
DC = 3072

GROUP = 4
TILE = GROUP * S
WIN = 208
STEP = 192
ONES = 16

eps_norm = 1e-06
keep_scale = 4.0 / 3.0
f32 = jnp.float32
bf16 = jnp.bfloat16
MIB = 1024 * 1024


def resident(shape):
    zeros = (0,) * len(shape)
    return pl.BlockSpec(shape, lambda *_: zeros, pipeline_mode=pl.Buffered(1))


def smem():
    return pl.BlockSpec(memory_space=pltpu.SMEM)


def anywhere():
    return pl.BlockSpec(memory_space=pl.ANY)


def call(kernel, after, in_specs, args, vmem, **rest):
    count = len(args)

    def body(*refs):
        kernel(*refs[:count], *refs[count + len(after) :])

    return pl.pallas_call(
        body,
        in_specs=list(in_specs) + [anywhere()] * len(after),
        compiler_params=pltpu.CompilerParams(vmem_limit_bytes=vmem * MIB),
        **rest,
    )(*args, *after)


def kept(skip, crop, branch):
    return skip[crop, branch].astype(f32) * keep_scale


def dot(a, b):
    return jnp.dot(a, b, preferred_element_type=f32)


def dot_nt(a, b):
    return lax.dot_general(a, b, (((1,), (1,)), ((), ())), preferred_element_type=f32)


def gelu_and_slope(z):
    phi = 0.5 * (1.0 + lax.erf(z * 0.7071067811865476))
    return z * phi, phi + z * jnp.exp(-0.5 * z * z) * 0.3989422804014327


def normalize(v):
    center = v - jnp.mean(v, axis=-1, keepdims=True)
    inv = lax.rsqrt(jnp.mean(center * center, axis=-1, keepdims=True) + eps_norm)
    return center * inv, inv


def join(values, axis, total):
    out, start = None, 0
    for v in values:
        pads = [(0, 0)] * v.ndim
        pads[axis] = (start, total - start - v.shape[axis])
        start += v.shape[axis]
        v = jnp.pad(v, pads)
        out = v if out is None else out + v
    return out


def per_row(values, shape, start=0):
    rows = lax.broadcasted_iota(jnp.int32, shape, 0) + start
    out = jnp.broadcast_to(values[GROUP - 1], shape)
    for c in range(GROUP - 2, -1, -1):
        out = jnp.where(rows < (c + 1) * S, values[c], out)
    return out


def crop_sum(read, c):
    lo, hi = c * S, (c + 1) * S
    base = c * STEP
    width = read(base, 8).shape[1]
    total = jnp.sum(read(base + 16, STEP - 16), axis=0, keepdims=True)
    for piece in (base, base + STEP):
        rows = lax.broadcasted_iota(jnp.int32, (16, width), 0) + piece
        ok = (rows >= lo) & (rows < hi)
        total += jnp.sum(jnp.where(ok, read(piece, 16), 0.0), axis=0, keepdims=True)
    return total


def window_matrix(c, shape):
    return jnp.where(
        lax.broadcasted_iota(jnp.int32, shape, 0) == lax.broadcasted_iota(jnp.int32, shape, 1) + 4 * c, 1.0, 0.0
    ).astype(bf16)


def token_forward_kernel(skip, x, wu, wd, bu, bd, vecs, x1_out, h2, act, slope, wu_out, wd_out, h1, x1, wut, wdt, bdt):
    i = pl.program_id(0)

    @pl.when(i == 0)
    def _():
        for c in range(GROUP):
            move = window_matrix(c, (WIN, S))
            wu_out[c] = dot(move, wu[...]).astype(bf16)
            wut[c] = lax.dot_general(
                wu[...], move, (((0,), (1,)), ((), ())), preferred_element_type=f32
            ).astype(bf16)
            wd_out[c] = dot_nt(wd[...], move).astype(bf16)
            wdt[c] = dot_nt(move, wd[...]).astype(bf16)
            bdt[c] = jnp.sum(move.astype(f32) * bd[...], axis=1, keepdims=True)

    tokens = x[...].astype(f32)
    normed, _ = normalize(tokens)
    h1[...] = (normed * vecs[0:1, :] + vecs[1:2, :]).astype(bf16)
    x1[...] = tokens

    def lift(c):
        return dot(wut[c], h1[pl.ds(c * STEP, WIN), :]) + bu[...]

    later = lift(0)
    for c in range(GROUP):
        lifted, later = later, lift(c + 1) if c + 1 < GROUP else None
        value, grad = gelu_and_slope(lifted)
        value = value.astype(bf16)
        act[c] = value
        slope[c] = grad.astype(bf16)
        mixed = dot(wdt[c], value) + bdt[c]
        x1[pl.ds(c * STEP, WIN), :] += kept(skip, i * GROUP + c, 0) * mixed
    x1_out[...] = x1[...].astype(bf16)
    normed, _ = normalize(x1[...])
    h2[...] = (normed * vecs[2:3, :] + vecs[3:4, :]).astype(bf16)


def token_forward(skip, x, wu, wd, bu, bd, vecs, after=()):
    rows = x.shape[0]
    crops = rows // S
    tile = pl.BlockSpec((TILE, D), lambda i: (i, 0))
    hidden = pl.BlockSpec((GROUP, DS, D), lambda i: (i, 0, 0))
    moved = [(GROUP, WIN, DS), (GROUP, DS, WIN)]
    return call(
        token_forward_kernel,
        after,
        [
            smem(),
            tile,
            resident((S, DS)),
            resident((DS, S)),
            resident((DS, 1)),
            resident((1, S)),
            resident((4, D)),
        ],
        (skip, x, wu, wd, bu, bd, vecs),
        vmem=50,
        grid=(rows // TILE,),
        out_specs=[tile, tile, hidden, hidden] + [pl.BlockSpec(m, lambda i: (0, 0, 0)) for m in moved],
        out_shape=[
            jax.ShapeDtypeStruct((rows, D), bf16),
            jax.ShapeDtypeStruct((rows, D), bf16),
            jax.ShapeDtypeStruct((crops, DS, D), bf16),
            jax.ShapeDtypeStruct((crops, DS, D), bf16),
        ]
        + [jax.ShapeDtypeStruct(m, bf16) for m in moved],
        scratch_shapes=[
            pltpu.VMEM((TILE, D), bf16),
            pltpu.VMEM((TILE, D), f32),
            pltpu.VMEM((GROUP, DS, WIN), bf16),
            pltpu.VMEM((GROUP, WIN, DS), bf16),
            pltpu.VMEM((GROUP, WIN, 1), f32),
        ],
        cost_estimate=pl.CostEstimate(
            flops=20 * rows * DS * D, bytes_accessed=rows * D * 12, transcendentals=0
        ),
        name="token_forward",
    )


def hidden_kernel(h2, up, bias, act_low, act_high, z_out, sums):
    i = pl.program_id(0)
    chunk = 512
    count = DC // chunk

    def hidden(j):
        cols = pl.ds(j * chunk, chunk)
        return dot(h2[...], up[:, cols]) + bias[:, cols]

    later = hidden(0)
    for j in range(count):
        cols = pl.ds(j * chunk, chunk)
        z, later = later, hidden(j + 1) if j + 1 < count else None
        z_out[:, cols] = z.astype(bf16)
        value = z * (0.5 * (1.0 + lax.erf(z * 0.7071067811865476)))
        half, k = divmod(j, count // 2)
        (act_low, act_high)[half][:, pl.ds(k * chunk, chunk)] = value.astype(bf16)
        for c in range(GROUP):
            sums[pl.ds(i * GROUP + c, 1), cols] = crop_sum(lambda a, n: value[a : a + n], c)


def hidden_forward(h2, up, bias, after=()):
    rows = h2.shape[0]
    grid = rows // TILE
    half = pl.BlockSpec((TILE, DC // 2), lambda i: (i, 0))
    return call(
        hidden_kernel,
        after,
        [pl.BlockSpec((TILE, D), lambda i: (i, 0)), resident((D, DC)), resident((1, DC))],
        (h2, up, bias),
        vmem=60,
        grid=(grid,),
        out_specs=[
            half,
            half,
            pl.BlockSpec((TILE, DC), lambda i: (i, 0)),
            pl.BlockSpec((grid * GROUP, DC), lambda i: (0, 0)),
        ],
        out_shape=[
            jax.ShapeDtypeStruct((rows, DC // 2), bf16),
            jax.ShapeDtypeStruct((rows, DC // 2), bf16),
            jax.ShapeDtypeStruct((rows, DC), bf16),
            jax.ShapeDtypeStruct((grid * GROUP, DC), f32),
        ],
        cost_estimate=pl.CostEstimate(
            flops=3 * rows * D * DC, bytes_accessed=rows * DC * 4, transcendentals=0
        ),
        name="hidden_forward",
    )


def output_kernel(skip, act_low, act_high, down, x1, bias, cotangent, out, scaled, pooled):
    i = pl.program_id(0)
    scale = per_row([kept(skip, i * GROUP + c, 1) for c in range(GROUP)], (TILE, 1))
    branch = dot(act_low[...], down[pl.ds(0, DC // 2), :]) + bias[...]
    branch += dot(act_high[...], down[pl.ds(DC // 2, DC // 2), :])
    y = x1[...].astype(f32) + scale * branch
    out[...] = y.astype(bf16)
    scaled[...] = (scale * cotangent[...].astype(f32)).astype(bf16)
    for c in range(GROUP):
        pooled[pl.ds(i * GROUP + c, 1), :] = crop_sum(lambda a, n: y[a : a + n], c) * (1.0 / S)


def output_forward(skip, act_low, act_high, down, x1, bias, cotangent, after=()):
    rows = x1.shape[0]
    grid = rows // TILE
    tile = pl.BlockSpec((TILE, D), lambda i: (i, 0))
    half = pl.BlockSpec((TILE, DC // 2), lambda i: (i, 0))
    return call(
        output_kernel,
        after,
        [smem(), half, half, resident((DC, D)), tile, resident((1, D)), tile],
        (skip, act_low, act_high, down, x1, bias, cotangent),
        vmem=60,
        grid=(grid,),
        out_specs=[tile, tile, pl.BlockSpec((grid * GROUP, D), lambda i: (0, 0))],
        out_shape=[
            jax.ShapeDtypeStruct((rows, D), bf16),
            jax.ShapeDtypeStruct((rows, D), bf16),
            jax.ShapeDtypeStruct((grid * GROUP, D), f32),
        ],
        cost_estimate=pl.CostEstimate(
            flops=2 * rows * D * DC, bytes_accessed=rows * DC * 2 + rows * D * 10, transcendentals=0
        ),
        name="output_forward",
    )


def lane_blocks(rows):
    count = max(rows // 768, 1)
    return [(k * 768, 768 if k < count - 1 else rows - 768 * (count - 1)) for k in range(count)]


def hidden_backward_kernel(
    skip, where, cotangent, differ, h2, down, z, gz, dw_own, dw_other, db, sums, grad, h2t
):
    j = pl.program_id(0)
    blocks = lane_blocks(h2.shape[0])

    @pl.when(j == 0)
    def _():
        total = jnp.zeros((1, D), f32)
        for i in range(cotangent.shape[0] // TILE):
            rows = pl.ds(i * TILE, TILE)
            scale = per_row([kept(skip, i * GROUP + c, 1) for c in range(GROUP)], (TILE, 1))
            shift = per_row([differ[pl.ds(i * GROUP + c, 1), :] for c in range(GROUP)], (TILE, D))
            value = (scale * (cotangent[rows, :].astype(f32) + (8.0 / S) * shift)).astype(bf16)
            grad[rows, :] = value
            total += jnp.sum(value.astype(f32), axis=0, keepdims=True)
        sums[...] = total
        square = (D, D)
        same = lax.broadcasted_iota(jnp.int32, square, 0) == lax.broadcasted_iota(jnp.int32, square, 1)
        eye = jnp.where(same, 1.0, 0.0).astype(bf16)
        for start, size in blocks:
            h2t[:, pl.ds(start, size)] = dot_nt(eye, h2[pl.ds(start, size), :]).astype(bf16)

    def first(b):
        start, size = blocks[b]
        return dot_nt(grad[pl.ds(start, size), :], down[...])

    dw = db_sum = None
    later = first(0)
    for b, (start, size) in enumerate(blocks):
        rows = pl.ds(start, size)
        part, later = later, first(b + 1) if b + 1 < len(blocks) else None
        hidden = z[rows, :].astype(f32)
        slope = (
            0.5 * (1.0 + lax.erf(hidden * 0.7071067811865476))
            + hidden * jnp.exp(-0.5 * hidden * hidden) * 0.3989422804014327
        )
        part = part * slope
        added = jnp.sum(part, axis=0, keepdims=True)
        db_sum = added if db_sum is None else db_sum + added
        part = part.astype(bf16)
        gz[rows, :] = part
        added = dot(h2t[:, rows], part)
        dw = added if dw is None else dw + added
    db[...] = db_sum
    unit = dw_own.shape[1]
    dw = dw.reshape(D // (2 * unit), 2, unit, dw.shape[1])
    dw_own[...] = jnp.where(where[0] == 0, dw[:, 0], dw[:, 1]).astype(bf16)
    dw_other[...] = jnp.where(where[0] == 0, dw[:, 1], dw[:, 0]).astype(bf16)


def hidden_backward(skip, core, cotangent, differ, h2, down, z, unit, after=()):
    rows = cotangent.shape[0]
    chunk = 512
    grads = (D // (2 * unit), unit)
    wide = pl.BlockSpec((rows, chunk), lambda j: (0, j))
    return call(
        hidden_backward_kernel,
        after,
        [
            smem(),
            smem(),
            resident((rows, D)),
            resident(differ.shape),
            resident((rows, D)),
            pl.BlockSpec((chunk, D), lambda j: (j, 0)),
            wide,
        ],
        (skip, jnp.reshape(core, (1,)).astype(jnp.int32), cotangent, differ, h2, down, z),
        vmem=52,
        grid=(DC // chunk,),
        out_specs=[
            wide,
            pl.BlockSpec(grads + (chunk,), lambda j: (0, 0, j)),
            pl.BlockSpec(grads + (chunk,), lambda j: (0, 0, j)),
            pl.BlockSpec((1, chunk), lambda j: (0, j)),
            pl.BlockSpec((1, D), lambda j: (0, 0)),
        ],
        out_shape=[
            jax.ShapeDtypeStruct((rows, DC), bf16),
            jax.ShapeDtypeStruct(grads + (DC,), bf16),
            jax.ShapeDtypeStruct(grads + (DC,), bf16),
            jax.ShapeDtypeStruct((1, DC), f32),
            jax.ShapeDtypeStruct((1, D), f32),
        ],
        scratch_shapes=[pltpu.VMEM((rows, D), bf16), pltpu.VMEM((D, rows), bf16)],
        cost_estimate=pl.CostEstimate(
            flops=4 * rows * D * DC, bytes_accessed=rows * DC * 4, transcendentals=0
        ),
        name="hidden_backward",
    )


def norm_back(grad, gain, normed, inv):
    scaled = grad * gain
    return inv * (
        scaled
        - jnp.mean(scaled, axis=-1, keepdims=True)
        - normed * jnp.mean(scaled * normed, axis=-1, keepdims=True)
    )


def last_backward_kernel(
    skip, gz, up, x1, cotangent, differ, x, act, slope, wd, wu, vecs, *rest, begin, first
):
    start, (out, dwd, dwu, sums, gh2, gx1, gv, h1, gh1) = rest[:-9], rest[-9:]
    i = pl.program_id(0)

    @pl.when(i == 0)
    def _():
        if first:
            dwd[...] = jnp.zeros_like(dwd)
            dwu[...] = jnp.zeros_like(dwu)
            sums[...] = jnp.zeros_like(sums)
        else:
            dwd[...] = start[1][...]
            dwu[...] = start[2][...]
            sums[...] = start[3][...]

    i += begin

    def add(row, value):
        sums[row : row + 1, :] += jnp.sum(value, axis=0, keepdims=True)

    block = TILE // 2
    for p in range(2):
        rows = pl.ds(p * block, block)
        gh2[rows, :] = dot_nt(gz[rows, :], up[...])
    normed_one, inv_one = normalize(x[...].astype(f32))
    h1[...] = (normed_one * vecs[0:1, :] + vecs[1:2, :]).astype(bf16)
    for p in range(2):
        rows = pl.ds(p * block, block)
        grad = gh2[rows, :]
        normed, inv = normalize(x1[rows, :].astype(f32))
        add(2, grad * normed)
        add(3, grad)
        shift = per_row(
            [differ[pl.ds(i * GROUP + c, 1), :] for c in range(GROUP)], (block, D), start=p * block
        )
        value = (
            cotangent[rows, :].astype(f32)
            + (8.0 / S) * shift
            + norm_back(grad, vecs[2:3, :], normed, inv)
        )
        gx1[rows, :] = value
        scale = per_row(
            [kept(skip, i * GROUP + c, 0) for c in range(GROUP)], (block, 1), start=p * block
        )
        gv[rows, :] = (scale * value).astype(bf16)

    gh1[...] = jnp.zeros_like(gh1)
    ones = jnp.ones((ONES, D), bf16)

    def back(c):
        return dot(wd[c], gv[pl.ds(c * STEP, WIN), :])

    later = back(0)
    for c in range(GROUP):
        rows = pl.ds(c * STEP, WIN)
        grad, later = later, back(c + 1) if c + 1 < GROUP else None
        dwd[c] += dot_nt(jnp.concatenate([act[c], ones], axis=0), gv[rows, :])
        gu = (grad * slope[c].astype(f32)).astype(bf16)
        dwu[c] += dot_nt(jnp.concatenate([h1[rows, :], ones], axis=0), gu)
        gh1[rows, :] += dot(wu[c], gu)
    grad = gh1[...]
    add(0, grad * normed_one)
    add(1, grad)
    out[...] = gx1[...] + norm_back(grad, vecs[0:1, :], normed_one, inv_one)


def last_backward(
    skip, gz, up, x1, cotangent, differ, x, act, slope, wd, wu, vecs, begin, count, before=None, after=()
):
    rows = x.shape[0]
    tile = pl.BlockSpec((TILE, D), lambda i: (i + begin, 0))
    hidden = pl.BlockSpec((GROUP, DS, D), lambda i: (i + begin, 0, 0))
    shapes = [(GROUP, DS + ONES, WIN), (GROUP, WIN + ONES, DS), (4, D)]
    extra = () if before is None else tuple(before)
    return call(
        functools.partial(last_backward_kernel, begin=begin, first=before is None),
        after,
        [
            smem(),
            pl.BlockSpec((TILE, DC), lambda i: (i + begin, 0)),
            resident((D, DC)),
            tile,
            tile,
            resident(differ.shape),
            tile,
            hidden,
            hidden,
            resident((GROUP, DS, WIN)),
            resident((GROUP, WIN, DS)),
            resident((4, D)),
        ]
        + ([] if before is None else [anywhere()] + [resident(s) for s in shapes]),
        (skip, gz, up, x1, cotangent, differ, x, act, slope, wd, wu, vecs) + extra,
        vmem=48,
        grid=(count,),
        out_specs=[
            tile,
            pl.BlockSpec(shapes[0], lambda i: (0, 0, 0)),
            pl.BlockSpec(shapes[1], lambda i: (0, 0, 0)),
            pl.BlockSpec(shapes[2], lambda i: (0, 0)),
        ],
        out_shape=[jax.ShapeDtypeStruct((rows, D), f32)] + [jax.ShapeDtypeStruct(s, f32) for s in shapes],
        scratch_shapes=[
            pltpu.VMEM((TILE, D), f32),
            pltpu.VMEM((TILE, D), f32),
            pltpu.VMEM((TILE, D), bf16),
            pltpu.VMEM((TILE, D), bf16),
            pltpu.VMEM((TILE, D), f32),
        ],
        input_output_aliases={} if before is None else {12: 0},
        cost_estimate=pl.CostEstimate(
            flops=count * TILE * (2 * D * DC + 20 * DS * D),
            bytes_accessed=count * TILE * (DC * 2 + D * 24),
            transcendentals=0,
        ),
        name="last_backward",
    )


def merge_kernel(where, low, high, low_in, high_in, sums, shift, *outs):
    i = pl.program_id(0)
    half = pl.num_programs(0) // 2
    *outs, over = outs
    over[...] = jnp.zeros_like(over)
    for k, out in enumerate(outs):
        place = where[1] ^ k
        added = dot(sums[place, 0], shift[...])
        own = jnp.where(i < half, low[place, 0], high[place, 0]).astype(f32)
        got = jnp.where(i < half, low_in[place], high_in[place]).astype(f32)
        out[0] = (own + got + added).astype(bf16)


def merge(core, at_xy, plane, low, high, low_in, high_in, sums, shift):
    half, _, rows, _ = low.shape
    steps = half // plane
    first = lambda i: jnp.minimum(i, steps - 1)
    second = lambda i: jnp.maximum(i - steps, 0)
    return pl.pallas_call(
        merge_kernel,
        grid_spec=pltpu.PrefetchScalarGridSpec(
            num_scalar_prefetch=1,
            grid=(2 * steps,),
            in_specs=[
                pl.BlockSpec((plane, 1, rows, D), lambda i, w: (first(i), w[0], 0, 0)),
                pl.BlockSpec((plane, 1, rows, D), lambda i, w: (second(i), w[0], 0, 0)),
                pl.BlockSpec((plane, rows, D), lambda i, w: (first(i), 0, 0)),
                pl.BlockSpec((plane, rows, D), lambda i, w: (second(i), 0, 0)),
                pl.BlockSpec((plane, 1) + sums.shape[2:], lambda i, w: (i, w[0], 0, 0)),
                pl.BlockSpec(shift.shape, lambda i, w: (0, 0)),
            ],
            out_specs=[pl.BlockSpec((1, rows, D), lambda i, w: (i, 0, 0))] * plane
            + [pl.BlockSpec((8, 128), lambda i, w: (0, 0))],
        ),
        out_shape=[jax.ShapeDtypeStruct((2 * steps, rows, D), bf16)] * plane
        + [jax.ShapeDtypeStruct((8, 128), f32)],
        compiler_params=pltpu.CompilerParams(vmem_limit_bytes=60 * MIB),
        name="merge",
    )(jnp.stack([core, at_xy]).astype(jnp.int32), low, high, low_in, high_in, sums, shift)


def place_kernel(where, *refs, pieces, side):
    out, held, sems = refs[-3:]
    kz = 2 * side
    copies = []
    for plane in range(kz):
        for k, (column, places) in enumerate(pieces):
            own, other = refs[2 * k], refs[2 * k + 1]
            rows, cols = own.shape[-2:]
            for index, (z, y, x) in enumerate(places):
                if z != plane:
                    continue
                chip = ((where[0] ^ z) * side + (where[1] ^ y)) * side + (where[2] ^ x)
                if rows % 16 == 0:
                    for ref, core in ((own, where[3]), (other, 1 - where[3])):
                        start = pl.multiple_of((chip * 2 + core) * rows, rows)
                        held[pl.ds(start, rows), pl.ds(column, cols)] = ref[index]
                else:
                    both = [own[index].astype(f32), other[index].astype(f32)]
                    low = jnp.where(where[3] == 0, both[0], both[1])
                    high = jnp.where(where[3] == 0, both[1], both[0])
                    start = pl.multiple_of(chip * 2 * rows, 2 * rows)
                    value = jnp.concatenate([low, high], axis=0).astype(bf16)
                    held[pl.ds(start, 2 * rows), pl.ds(column, cols)] = value
        size = held.shape[0] // kz
        part = pl.ds(pl.multiple_of((where[0] ^ plane) * size, size), size)
        copies.append(pltpu.make_async_copy(held.at[part], out.at[part], sems.at[plane]))
        copies[-1].start()
    for copy in copies:
        copy.wait()


def behind(value, *others):
    return lax.optimization_barrier((value,) + others)[0]


class Net:
    def __init__(self, n):
        chips = n // 2
        side = 1
        while 2 * side * side * side < chips:
            side *= 2
        if 2 * side * side * side != chips:
            raise ValueError("unknown slice")
        self.n, self.side, self.chips = n, side, chips
        self.core = [1]
        self.xy = [2 * k for k in range(1, side * side)]
        self.x = [2 * k for k in range(1, side)]
        self.y = [2 * side * k for k in range(1, side)]
        self.z = [2 * side * side * k for k in range(1, 2 * side)]
        self.me = lax.axis_index("dp")
        self.at_core = self.me % 2
        self.at_xy = (self.me // 2) % (side * side)
        self.at_x = (self.me // 2) % side
        self.at_y = (self.me // (2 * side)) % side
        self.at_z = self.me // (2 * side * side)

    def swap(self, value, offset):
        return lax.ppermute(value, "dp", [(i, i ^ offset) for i in range(self.n)])

    def spread(self, value, offsets):
        return jnp.stack([value] + [self.swap(value, o) for o in offsets])

    def gather_small(self, value, beside=(), chips=False):
        held = value
        order = np.array([0], np.int64)
        steps = []
        for k, offsets in enumerate((self.z, self.xy) if chips else (self.z, self.xy, self.core)):
            held = self.spread(held, offsets)
            if k < len(beside):
                held = behind(held, beside[k])
            steps.append(held)
            order = (np.array([0] + offsets)[:, None] + order[None, :]).reshape(-1)
        return held.reshape((-1,) + value.shape), order, steps

    def plane(self, stacked):
        side = self.side
        places = [(z, 0, 0) for z in range(2 * side)]
        out = [(stacked, places, 0)]
        for k, offset in enumerate(self.xy):
            y, x = divmod(k + 1, side)
            out.append((self.swap(stacked, offset), [(z, y, x) for z, _, _ in places], 0))
        return out

    def place(self, parts, others, after=()):
        side, kz = self.side, 2 * self.side
        rows = parts[0][0].shape[1]
        width = max(column + blocks.shape[2] for blocks, _, column in parts)
        pairs = [(blocks, other) for (blocks, _, _), other in zip(parts, others)]
        shape = (self.n * rows, width)
        if rows % 8 == 0:
            pieces = [(column, places) for _, places, column in parts]
            where = jnp.stack([self.at_z, self.at_y, self.at_x, self.at_core]).astype(jnp.int32)
            inputs = [v for pair in pairs for v in pair]
            return call(
                functools.partial(place_kernel, pieces=pieces, side=side),
                after,
                [smem()] + [pl.BlockSpec(memory_space=pltpu.VMEM)] * len(inputs),
                (where, *inputs),
                vmem=50,
                out_specs=anywhere(),
                out_shape=jax.ShapeDtypeStruct(shape, bf16),
                scratch_shapes=[pltpu.VMEM(shape, bf16), pltpu.SemaphoreType.DMA((kz,))],
                name="place",
            )
        columns = {}
        for (blocks, places, column), pair in zip(parts, pairs):
            columns.setdefault(column, []).extend(
                (core, place, pair[core][k]) for k, place in enumerate(places) for core in (0, 1)
            )
        out = []
        for column in sorted(columns):
            blocks = sorted(columns[column], key=lambda b: (b[1], b[0]))
            held = jnp.stack([b[2] for b in blocks]).reshape(kz, side, side, 2, rows, -1)
            for axis, at in enumerate((self.at_z, self.at_y, self.at_x, self.at_core)):
                held = jnp.take(held, jnp.arange(held.shape[axis]) ^ at, axis=axis)
            out.append(held.reshape(shape[0], -1))
        return jnp.concatenate(out, axis=1)

    def pick(self, value, index, axis):
        return lax.dynamic_index_in_dim(value, index, axis, keepdims=False)

    def start_axis(self, value, axis, at, offsets):
        own = self.pick(value, at, axis)
        return [own] + [
            self.swap(self.pick(value, at ^ (k + 1), axis).astype(bf16), o) for k, o in enumerate(offsets)
        ]

    def finish_axis(self, parts):
        parts = [p.astype(f32) for p in parts]
        while len(parts) > 1:
            parts = [parts[k] + parts[k + 1] for k in range(0, len(parts), 2)]
        return parts[0]

    def scatter_small(self, value):
        kz, k = 2 * self.side, self.side
        value = value.reshape(kz, k * k, 2, -1)
        value = self.finish_axis(self.start_axis(value, 2, self.at_core, self.core)).astype(bf16)
        value = self.finish_axis(self.start_axis(value, 1, self.at_xy, self.xy)).astype(bf16)
        return self.finish_axis(self.start_axis(value, 0, self.at_z, self.z))


def per_device(
    tokens,
    cotangent,
    skip_mask,
    pair_index,
    patch_up,
    patch_down,
    channel_up,
    channel_down,
    patch_upbias,
    patch_downbias,
    first_gain,
    first_shift,
    second_gain,
    second_shift,
    channel_upbias,
    channel_downbias,
    devices,
):
    net = Net(devices)
    chips = devices // 2
    core = net.at_core
    rows = tokens.shape[0]
    crops = rows // S
    unit_d = D // devices
    unit_h = DC // devices
    kz, kxy = 2 * net.side, net.side * net.side

    small = [
        patch_up, patch_down, first_gain, first_shift, second_gain, second_shift, channel_upbias, channel_downbias,
    ]
    sizes = [v.shape[0] for v in small]
    length = sum(sizes)
    padded = -(-length // 1024) * 1024
    packed = join(small, 0, padded)
    every, order, steps = net.gather_small(packed)
    channel_up = behind(channel_up, steps[0])
    skip_mask, pair_index, patch_upbias, patch_downbias = lax.optimization_barrier(
        (skip_mask, pair_index, patch_upbias, patch_downbias, steps[1])
    )[:4]
    in_order = (jnp.arange(devices)[:, None] ^ net.me) == jnp.asarray(order, jnp.int32)[None, :]
    every = dot(in_order.astype(bf16), every).astype(bf16)
    ends = np.cumsum([0] + sizes)
    up_token = every[:, : ends[1]].reshape(S, DS)
    down_token = every[:, ends[1] : ends[2]].reshape(DS, S)
    vecs = every[:, ends[2] : ends[6]].astype(f32).reshape(devices, 4, unit_d).transpose(1, 0, 2).reshape(4, D)
    bias_hidden = every[:, ends[6] : ends[7]].astype(f32).reshape(1, DC)
    bias_out = every[:, ends[7] : ends[8]].astype(f32).reshape(1, D)

    up_stack = net.spread(channel_up.reshape(unit_d, DC), net.z)
    down_stack = net.spread(behind(channel_down, up_stack).reshape(unit_h, D), net.z)
    up_parts = net.plane(up_stack)

    x1, h2, act_t, slope_t, up_pad, down_pad = token_forward(
        skip_mask,
        tokens,
        up_token,
        down_token,
        patch_upbias.astype(f32).reshape(DS, 1),
        patch_downbias.astype(f32).reshape(1, S),
        vecs,
        after=(up_stack, bias_hidden, bias_out),
    )
    up_parts = [(behind(blocks, h2, down_stack), places, column) for blocks, places, column in up_parts]
    up = net.place(up_parts, [net.swap(blocks, 1) for blocks, _, _ in up_parts])
    down_parts = net.plane(behind(down_stack, h2))
    other_pairs, other_skip = net.swap(pair_index, 1), net.swap(skip_mask[:, 1], 1)
    act_low, act_high, z, act_sums = hidden_forward(h2, up, bias_hidden)
    down_parts = [(behind(blocks, act_sums), places, column) for blocks, places, column in down_parts]
    down = net.place(down_parts, [net.swap(blocks, 1) for blocks, _, _ in down_parts])
    outputs, scaled, pooled = output_forward(skip_mask, act_low, act_high, down, x1, bias_out, cotangent)
    other_pairs, other_skip = behind(other_pairs, act_sums), behind(other_skip, act_sums)

    chip_sums = act_sums.astype(bf16)
    chip_sums = jnp.concatenate([chip_sums, net.swap(chip_sums, 1)]).T.reshape(chips, 2, unit_h, 2 * crops)

    def grad_down(act):
        value = lax.dot_general(act, scaled, (((0,), (0,)), ((), ())), preferred_element_type=f32)
        return value.astype(bf16).reshape(chips // 2, 2, unit_h, D)

    low, high = grad_down(act_low), grad_down(act_high)
    every, order, steps = net.gather_small(pooled.astype(bf16), beside=(low, high), chips=True)
    every = every.reshape(-1, D)
    every_other = net.swap(every, 1)
    low, high = behind(low, steps[1]), behind(high, steps[1])
    received = [net.swap(net.pick(v, 1 - core, 1), 1) for v in (low, high)]
    codes = (order[:, None] * crops + np.arange(crops)[None, :]).reshape(1, -1)
    flip = net.me.astype(jnp.int32) * crops

    def find(index):
        code = (index.reshape(-1, 1) ^ flip) - jnp.asarray(codes, jnp.int32)
        return dot((code == 0).astype(bf16), every) + dot((code == crops).astype(bf16), every_other)

    partner = find(jnp.stack([pair_index, other_pairs]))
    differ = pooled - partner[:crops]
    own_code = jnp.stack([net.me, net.me ^ 1]).astype(jnp.int32)[:, None] * crops + jnp.arange(crops, dtype=jnp.int32)
    chip_differ = find(own_code) - partner
    losses = 2.0 * jnp.sum(differ * differ, axis=1)

    chip_keep = jnp.stack([skip_mask[:, 1], other_skip]).astype(f32).reshape(-1, 1) * keep_scale
    chip_shift = (chip_keep * (8.0 / S) * chip_differ).astype(bf16)
    *down_sum, over = merge(core, net.at_xy, kxy, low, high, *received, chip_sums, chip_shift)
    down_parts = [down_sum[0]] + [net.swap(v, o) for v, o in zip(down_sum[1:], net.xy)]

    gz, up_own, up_other, grad_bias_hidden, grad_bias_out = hidden_backward(
        skip_mask, core, cotangent, differ, h2, down, z, unit_d, after=(over,)
    )
    down_sum = net.finish_axis(down_parts)
    up_other = net.swap(behind(up_other, down_sum), 1)
    down_parts = net.start_axis(down_sum, 0, net.at_z, net.z)
    tiles = rows // TILE
    cuts = (0, 1, tiles)
    passed = (
        skip_mask, gz, up, x1, cotangent, differ, tokens, act_t, slope_t, down_pad, up_pad, vecs
    )
    done = last_backward(*passed, cuts[0], cuts[1] - cuts[0], after=(down_sum,))
    up_sum = (up_own.astype(f32) + behind(up_other, done[3]).astype(f32)).astype(bf16)
    down_grad = net.finish_axis([behind(v, done[3]) for v in down_parts]).reshape(-1)
    up_parts = net.start_axis(up_sum.reshape(kz, kxy, unit_d, DC), 1, net.at_xy, net.xy)
    grad_tokens, dwd, dwu, sums = last_backward(
        *passed, cuts[1], cuts[2] - cuts[1], before=done, after=(down_grad,)
    )
    up_sum = net.finish_axis([behind(v, sums) for v in up_parts])
    dwd, dwu, sums, up_sum = lax.optimization_barrier((dwd, dwu, sums, up_sum))
    up_parts = net.start_axis(up_sum, 0, net.at_z, net.z)
    up_grad = net.finish_axis(up_parts).reshape(-1)

    grad_patch_up = sum(dwu[c, 4 * c : 4 * c + S] for c in range(GROUP))
    grad_patch_down = sum(dwd[c, :DS, 4 * c : 4 * c + S] for c in range(GROUP))
    bias_up = sum(dwu[c, WIN] for c in range(GROUP))
    bias_down = sum(dwd[c, DS, 4 * c : 4 * c + S] for c in range(GROUP))
    scattered = [
        grad_patch_up, grad_patch_down, sums[0], sums[1], sums[2], sums[3], grad_bias_hidden, grad_bias_out
    ]
    scattered = [v.reshape(devices, -1) for v in scattered]
    scattered += [jnp.broadcast_to(v, (devices,) + v.shape) for v in (bias_up, bias_down)]
    total = sum(v.shape[1] for v in scattered)
    scattered = join([v.astype(bf16) for v in scattered], 1, -(-total // 1024) * 1024)
    own = net.scatter_small(scattered)
    ends = np.cumsum([0] + sizes + [DS, S])
    grads = [own[a:b] for a, b in zip(ends[:-1], ends[1:])]
    return (
        outputs, losses, grad_tokens, grads[0], grads[1], up_grad, down_grad, grads[8], grads[9], *grads[2:8],
    )


def solution(mesh):
    row, flat, whole = P("dp", None), P("dp"), P()
    return jax.shard_map(
        functools.partial(per_device, devices=mesh.shape["dp"]),
        mesh=mesh,
        in_specs=(row, row, row, flat, flat, flat, flat, flat, whole, whole) + (flat,) * 6,
        out_specs=(row, flat, row, flat, flat, flat, flat, whole, whole) + (flat,) * 6,
        check_vma=False,
    )
```
